256 devices in a mesh: gx: 16 (over y, x), gy: 2 (over core), gz: 8 (over z).
Axes of the slice: x: 4, y: 4, z: 8, core: 2. Of those that a mesh axis runs over, the one named last changes fastest.
Arguments:
- fields: float32 [8, 128, 256, 256], P(None, 'gz', 'gx', 'gy'), as said below
- col_cells: int32 [128], replicated, may hold values from 0 to 255, as said below
- col_num: int32 [128], replicated, may hold values from 0 to 63
- shear_sub: int32 [1], replicated, may hold values from 0 to 16383
Outputs:
- updated: float32 [8, 128, 256, 256], P(None, 'gz', 'gx', 'gy')
The draws below stay inside these ranges and needn't reach their ends.
Inputs may be any that keep to these rules, and one draw needn't show every extreme that they name: `col_cells`: the whole-cell shifts run over the whole azimuthal loop. The density fields[0] lies between 0.5 and 2.
All inputs are finite; a program needn't handle non-finite values.
Results may differ from the reference program's by a relative error of at most 0.0003.
Values sent between devices are 32-bit elements; how exact they have to be, the bound alone decides.
No kernel may reach another device: no remote copies, remote signals or barrier semaphores. Data moves between devices by JAX's collectives and lax.ppermute only.
A program may use at most 128 MiB of HBM per device.

```python
import math
import jax
import jax.numpy as jnp
from jax import lax

NF = 8
DEN = 64
NX = 128
NY = 256
NZ = 256


def draw_fields(key, part):
    key = jax.random.fold_in(key, 1)
    key_one, key_two = jax.random.split(key)
    density = jnp.exp(jax.random.uniform(key_one, (NX, NY, NZ), jnp.float32, math.log(0.5), math.log(2.0)))
    others = jnp.clip(0.4 * jax.random.normal(key_two, (NF - 1, NX, NY, NZ), jnp.float32), -1.2, 1.2)
    return jnp.concatenate([density[None], others], axis=0)


def draw_col_cells(key, part):
    key = jax.random.fold_in(key, 2)
    values = jax.random.randint(key, (NX,), 0, NY, dtype=jnp.int32)
    return values.at[0].set(0).at[NX - 1].set(NY - 1)


def draw_col_num(key, part):
    key = jax.random.fold_in(key, 3)
    values = jax.random.randint(key, (NX,), 0, DEN, dtype=jnp.int32)
    return values.at[1].set(0).at[NX - 2].set(DEN - 1)


def setup_inputs(seed: int = 0) -> dict:
    keys = jax.random.split(jax.random.key(seed), 5)
    return {
        "fields": draw_fields(jax.random.fold_in(keys[4], 71), 0),
        "col_cells": draw_col_cells(jax.random.fold_in(keys[4], 71), 0),
        "col_num": draw_col_num(jax.random.fold_in(keys[4], 71), 0),
        "shear_sub": jax.random.randint(keys[3], (1,), 0, NY * DEN).astype(jnp.int32),
    }


time_step = 0.2
gravity_rate = 4.0


def minmod(left, right):
    return 0.5 * (jnp.sign(left) + jnp.sign(right)) * jnp.minimum(jnp.abs(left), jnp.abs(right))


def divergence(values, speed, axis):
    length = values.shape[axis] - 4
    minus = lax.slice_in_dim(values, 1, length + 3, axis=axis) - lax.slice_in_dim(values, 0, length + 2, axis=axis)
    plus = lax.slice_in_dim(values, 2, length + 4, axis=axis) - lax.slice_in_dim(values, 1, length + 3, axis=axis)
    slope = minmod(minus, plus)
    left_state = lax.slice_in_dim(values, 1, length + 2, axis=axis) + 0.5 * lax.slice_in_dim(slope, 0, length + 1, axis=axis)
    right_state = lax.slice_in_dim(values, 2, length + 3, axis=axis) - 0.5 * lax.slice_in_dim(slope, 1, length + 2, axis=axis)
    face_speed = 0.5 * (lax.slice_in_dim(speed, 1, length + 2, axis=axis - 1) + lax.slice_in_dim(speed, 2, length + 3, axis=axis - 1))
    face_speed = jnp.expand_dims(face_speed, 0)
    flux = jnp.maximum(face_speed, 0.0) * left_state + jnp.minimum(face_speed, 0.0) * right_state
    return lax.slice_in_dim(flux, 1, length + 1, axis=axis) - lax.slice_in_dim(flux, 0, length, axis=axis)


def tendency(padded):
    density = padded[0]
    div_x = divergence(padded[:, :, 2:-2, 2:-2], (padded[1] / density)[:, 2:-2, 2:-2], 1)
    div_y = divergence(padded[:, 2:-2, :, 2:-2], (padded[2] / density)[2:-2, :, 2:-2], 2)
    div_z = divergence(padded[:, 2:-2, 2:-2, :], (padded[3] / density)[2:-2, 2:-2, :], 3)
    return div_x + div_y + div_z


def reference(fields, col_cells, col_num, shear_sub):
    columns = jnp.arange(-2, NX + 2, dtype=jnp.int32)
    source = columns % NX
    shear = shear_sub[0]
    total = DEN * col_cells[source] + col_num[source] + jnp.where(columns < 0, shear, 0) - jnp.where(columns >= NX, shear, 0)
    cells = (total // DEN) % NY
    frac = (total % DEN).astype(jnp.float32) / DEN
    rows = jnp.arange(NY, dtype=jnp.int32)
    first = (rows[None, :] - cells[:, None]) % NY
    second = (first - 1) % NY
    based = fields[:, source]
    upper_val = jnp.take_along_axis(based, first[None, :, :, None], axis=2)
    lower_val = jnp.take_along_axis(based, second[None, :, :, None], axis=2)
    remapped = (1.0 - frac)[None, :, None, None] * upper_val + frac[None, :, None, None] * lower_val
    padded = jnp.pad(remapped, ((0, 0), (0, 0), (2, 2), (0, 0)), mode="wrap")
    padded = jnp.pad(padded, ((0, 0), (0, 0), (0, 0), (2, 2)), mode="edge")
    interior = remapped[:, 2:-2]
    updated = interior - time_step * tendency(padded)
    height = gravity_rate * ((jnp.arange(NZ, dtype=jnp.int32).astype(jnp.float32) + 0.5) / NZ - 0.5)
    updated = updated.at[3].add(-time_step * height[None, None, :] * interior[0])
    return updated
```

```python
import jax
import jax.numpy as jnp
from jax import lax
from jax.experimental import pallas as pl
from jax.experimental.pallas import tpu as pltpu
from jax.sharding import PartitionSpec as P

DT = 0.2
GRAVITY = 4.0
NZ = 256
NB = 16
VMEM = pl.BlockSpec(memory_space=pltpu.VMEM)
SMEM = pl.BlockSpec(memory_space=pltpu.SMEM)


def shift_kernel(cells_ref, num_ref, shear_ref, src_ref, out_ref, line):
    gz = lax.axis_index("gz")
    last = lax.axis_size("gz") - 1
    half = lax.rem(lax.axis_index("gx"), 2)
    first_col = gz * 16 + half * 8
    shear = shear_ref[0]
    side = jnp.where(
        half == 1, jnp.where(gz == last, shear, 0), jnp.where(gz == 0, -shear, 0)
    )

    def one(col, extra, row):
        total = 64 * cells_ref[first_col + col] + num_ref[first_col + col] + extra
        cells = (total >> 6) & 255
        frac = (total & 63).astype(jnp.float32) * (1.0 / 64.0)
        line[0:8] = src_ref[15, col, 8:16]
        for b in range(16):
            line[8 + 16 * b : 24 + 16 * b] = src_ref[b, col]
        line[264:280] = src_ref[0, col]
        near = 1.0 - frac
        for m in range(32):
            start = ((8 * m - cells) & 255) + 8
            value = near * line[pl.ds(start, 8)] + frac * line[pl.ds(start - 1, 8)]
            out_ref[m // 2, pl.ds(pl.multiple_of(row + 8 * (m % 2), 8), 8)] = value

    @pl.loop(0, 8)
    def _(col):
        one(col, 0, 16 * col)

    @pl.loop(0, 2)
    def _(e):
        one(e + 6 * half, side, 160 + 16 * e)

    sub = lax.broadcasted_iota(jnp.int32, (8, 128), 0)
    top = sub < 4
    own = (sub < 2) | (sub >= 6)

    @pl.loop(0, 4)
    def _(c):
        for d in range(16):
            lo, hi = (d + 15) % 16, (d + 1) % 16
            a = pl.multiple_of(16 * c, 16)
            b = pl.multiple_of(16 * c + 64, 16)
            one_halo = jnp.where(top, out_ref[hi, pl.ds(a, 8)], out_ref[lo, pl.ds(a + 8, 8)])
            two_halo = jnp.where(top, out_ref[hi, pl.ds(b, 8)], out_ref[lo, pl.ds(b + 8, 8)])
            out_ref[d, pl.ds(pl.multiple_of(128 + 8 * c, 8), 8)] = jnp.where(
                own, one_halo, pltpu.roll(two_halo, 4, 0)
            )


def limited(a, b):
    return jnp.maximum(jnp.minimum(a, b), 0.0) + jnp.minimum(jnp.maximum(a, b), 0.0)


def face_difference(qs, vs):
    m2, m1, q, p1, p2 = qs
    vm, v, vp = vs
    d0, d1, d2, d3 = m1 - m2, q - m1, p1 - q, p2 - p1
    s0, s1, s2 = 0.5 * limited(d0, d1), 0.5 * limited(d1, d2), 0.5 * limited(d2, d3)
    a_lo, a_hi = 0.5 * (vm + v), 0.5 * (v + vp)
    lo = a_lo * jnp.where(a_lo > 0, m1 + s0, q - s1)
    hi = a_hi * jnp.where(a_hi > 0, q + s1, p1 - s2)
    return hi - lo


def update_kernel(t_ref, lo_ref, hi_ref, p_ref, out_ref, q_ref, vx_ref, vy_ref):
    gy = lax.axis_index("gy")
    lane = lax.broadcasted_iota(jnp.int32, (16, 128), 1)
    low_half = lane < 64
    zc = GRAVITY * (((lane + gy * 128).astype(jnp.float32) + 0.5) / NZ - 0.5)
    for f in range(8):
        for e in range(2):
            q_ref[f, e, 8:24] = lo_ref[f, 16 * e : 16 * e + 16]
            q_ref[f, 18 + e, 8:24] = hi_ref[f, 16 * e : 16 * e + 16]
        for h in range(2):
            for c in range(8):
                q_ref[f, 2 + 8 * h + c, 8:24] = t_ref[2 * f + h, 16 * c : 16 * c + 16]
            for c in range(4):
                tile = t_ref[2 * f + h, 128 + 8 * c : 136 + 8 * c]
                q_ref[f, 2 + 8 * h + c, 0:8] = tile
                q_ref[f, 2 + 8 * h + c, 24:32] = tile
                tile = pltpu.roll(tile, 4, 0)
                q_ref[f, 6 + 8 * h + c, 0:8] = tile
                q_ref[f, 6 + 8 * h + c, 24:32] = tile

    @pl.loop(1, 19)
    def _(x):
        vx_ref[x] = q_ref[1, x, 8:24] / q_ref[0, x, 8:24]

    @pl.loop(0, 16)
    def _(x):
        vy_ref[...] = q_ref[2, x + 2] / q_ref[0, x + 2]
        vys = [vy_ref[7 + k : 23 + k] for k in range(3)]
        vxs = [vx_ref[x + 1 + k] for k in range(3)]
        half, col = x // 8, lax.rem(x, 8)
        row = pl.multiple_of(16 * col, 16)

        def edges(f):
            q = q_ref[f, x + 2, 8:24]
            other = p_ref[2 * f + half, pl.ds(row, 16)]
            first = jnp.broadcast_to(q[:, 0:1], (16, 128))
            final = jnp.broadcast_to(q[:, 127:128], (16, 128))
            edge = jnp.where(gy == 0, first, final)
            return q, jnp.where(low_half == (gy == 0), other, edge)

        def shifted(q, p):
            return [
                pltpu.roll(jnp.where(lane >= 126, p, q), 2, 1),
                pltpu.roll(jnp.where(lane >= 127, p, q), 1, 1),
                q,
                pltpu.roll(jnp.where(lane < 1, p, q), 127, 1),
                pltpu.roll(jnp.where(lane < 2, p, q), 126, 1),
            ]

        q0, p0 = edges(0)
        q3, p3 = edges(3)
        vzs = shifted(q3 / q0, p3 / p0)[1:4]
        for f in range(8):
            q, p = edges(f)
            total = face_difference(shifted(q, p), vzs)
            total += face_difference([q_ref[f, x, 8:24], q_ref[f, x + 1, 8:24], q,
                                      q_ref[f, x + 3, 8:24], q_ref[f, x + 4, 8:24]], vxs)
            total += face_difference([q_ref[f, x + 2, 6 + k : 22 + k] for k in range(5)], vys)
            new = q - DT * total
            if f == 3:
                new -= DT * zc * q0
            out_ref[f, x] = new


def local(fields, col_cells, col_num, shear_sub):
    pieces = fields.reshape(NB, 8, 16, 128)
    lines = lax.all_to_all(pieces, "gx", 0, 0, tiled=True)
    send = pl.pallas_call(
        shift_kernel,
        out_shape=jax.ShapeDtypeStruct((NB, 192, 128), jnp.float32),
        in_specs=[SMEM, SMEM, SMEM, VMEM],
        out_specs=VMEM,
        scratch_shapes=[pltpu.VMEM((280, 128), jnp.float32)],
        compiler_params=pltpu.CompilerParams(vmem_limit_bytes=16 * 2**20),
        name="shift",
    )(col_cells, col_num, shear_sub, lines)
    t = lax.all_to_all(send, "gx", 0, 0, tiled=True)
    count = lax.axis_size("gz")
    up = [(i, (i + 1) % count) for i in range(count)]
    down = [(b, a) for a, b in up]
    by_half = t.reshape(8, 2, 192, 128)
    lo = lax.ppermute(by_half[:, 1, 160:], "gz", up)
    hi = lax.ppermute(by_half[:, 0, 160:], "gz", down)
    partner = lax.ppermute(t[:, :128], "gy", [(0, 1), (1, 0)])
    return pl.pallas_call(
        update_kernel,
        out_shape=jax.ShapeDtypeStruct((8, 16, 16, 128), jnp.float32),
        in_specs=[VMEM] * 4,
        out_specs=VMEM,
        scratch_shapes=[
            pltpu.VMEM((8, 20, 32, 128), jnp.float32),
            pltpu.VMEM((20, 16, 128), jnp.float32),
            pltpu.VMEM((32, 128), jnp.float32),
        ],
        compiler_params=pltpu.CompilerParams(vmem_limit_bytes=32 * 2**20),
        name="update",
    )(t, lo, hi, partner)


def solution(mesh):
    return jax.shard_map(
        local,
        mesh=mesh,
        in_specs=(P(None, "gz", "gx", "gy"), P(), P(), P()),
        out_specs=P(None, "gz", "gx", "gy"),
        check_vma=False,
    )
```

```python
import jax
import jax.numpy as jnp
from jax import lax
from jax.experimental import pallas as pl
from jax.experimental.pallas import tpu as pltpu
from jax.sharding import PartitionSpec as P

DT = 0.2
GRAVITY = 4.0
NZ = 256
NB = 16
VMEM = pl.BlockSpec(memory_space=pltpu.VMEM)
SMEM = pl.BlockSpec(memory_space=pltpu.SMEM)


def shift_kernel(cells_ref, num_ref, shear_ref, src_ref, out_ref, line):
    gz = lax.axis_index("gz")
    last = lax.axis_size("gz") - 1
    half = lax.rem(lax.axis_index("gx"), 2)
    first_col = gz * 16 + half * 8
    shear = shear_ref[0]
    side = jnp.where(
        half == 1, jnp.where(gz == last, shear, 0), jnp.where(gz == 0, -shear, 0)
    )

    def one(col, extra, row):
        total = 64 * cells_ref[first_col + col] + num_ref[first_col + col] + extra
        cells = (total >> 6) & 255
        frac = (total & 63).astype(jnp.float32) * (1.0 / 64.0)
        line[0:8] = src_ref[15, col, 8:16]
        for b in range(16):
            line[8 + 16 * b : 24 + 16 * b] = src_ref[b, col]
        line[264:280] = src_ref[0, col]
        near = 1.0 - frac
        for m in range(32):
            start = ((8 * m - cells) & 255) + 8
            value = near * line[pl.ds(start, 8)] + frac * line[pl.ds(start - 1, 8)]
            out_ref[m // 2, pl.ds(pl.multiple_of(row + 8 * (m % 2), 8), 8)] = value

    @pl.loop(0, 8)
    def _(col):
        one(col, 0, 16 * col)

    @pl.loop(0, 2)
    def _(e):
        one(e + 6 * half, side, 160 + 16 * e)

    sub = lax.broadcasted_iota(jnp.int32, (8, 128), 0)
    top = sub < 4
    own = (sub < 2) | (sub >= 6)

    @pl.loop(0, 4)
    def _(c):
        for d in range(16):
            lo, hi = (d + 15) % 16, (d + 1) % 16
            a = pl.multiple_of(16 * c, 16)
            b = pl.multiple_of(16 * c + 64, 16)
            one_halo = jnp.where(top, out_ref[hi, pl.ds(a, 8)], out_ref[lo, pl.ds(a + 8, 8)])
            two_halo = jnp.where(top, out_ref[hi, pl.ds(b, 8)], out_ref[lo, pl.ds(b + 8, 8)])
            out_ref[d, pl.ds(pl.multiple_of(128 + 8 * c, 8), 8)] = jnp.where(
                own, one_halo, pltpu.roll(two_halo, 4, 0)
            )


def limited(a, b):
    return jnp.maximum(jnp.minimum(a, b), 0.0) + jnp.minimum(jnp.maximum(a, b), 0.0)


def upwind(a, left, right):
    return a * jnp.where(a > 0, left, right)


def cells_of(t_ref, f, x):
    return t_ref[2 * f + x // 8, 16 * (x % 8) : 16 * (x % 8) + 16]


def ring_of(t_ref, f, x):
    c = x % 4
    tile = t_ref[2 * f + x // 8, 128 + 8 * c : 136 + 8 * c]
    if x % 8 >= 4:
        tile = pltpu.roll(tile, 4, 0)
    return jnp.concatenate([tile, cells_of(t_ref, f, x)], axis=0)


def inner_kernel(t_ref, out_ref, ax_ref, ay_ref):
    before = None
    for x in range(16):
        density = ring_of(t_ref, 0, x)
        inverse = 1.0 / density
        vy = ring_of(t_ref, 2, x) * inverse
        ay_ref[x] = 0.5 * (vy + pltpu.roll(vy, 1, 0))
        vx = cells_of(t_ref, 1, x) * inverse[8:]
        if x:
            ax_ref[x] = 0.5 * (vx + before)
        before = vx

    @pl.loop(0, 8)
    def _(f):
        qs, ds, fluxes, totals = {}, {}, {}, {}
        last = None
        for x in range(16):
            ring = ring_of(t_ref, f, x)
            d = ring - pltpu.roll(ring, 1, 0)
            h = 0.5 * limited(d, pltpu.roll(d, 23, 0))
            flux = upwind(ay_ref[x], pltpu.roll(ring + h, 1, 0), ring - h)
            totals[x] = (pltpu.roll(flux, 23, 0) - flux)[8:]
            q = ring[8:]
            qs[x] = q
            if x >= 1:
                ds[x] = q - qs[x - 1]
            if x >= 2:
                h = 0.5 * limited(ds[x - 1], ds[x])
                if x >= 3:
                    fluxes[x - 1] = upwind(ax_ref[x - 1], last, qs[x - 1] - h)
                last = qs[x - 1] + h
            if x >= 4:
                totals[x - 2] += fluxes[x - 1] - fluxes[x - 2]
            if x >= 2:
                out_ref[f, x - 2] = qs[x - 2] - DT * totals[x - 2]
        for x in (14, 15):
            out_ref[f, x] = qs[x] - DT * totals[x]


def height_kernel(t_ref, p_ref, acc_ref, out_ref, edge_ref, lo_ref, hi_ref):
    gy = lax.axis_index("gy")
    lane = lax.broadcasted_iota(jnp.int32, (16, 128), 1)
    first, final = lane == 0, lane == 127

    def parts(q, p, low):
        if low:
            below = jnp.where(first, q, pltpu.roll(q, 1, 1))
            above = pltpu.roll(jnp.where(first, p, q), 127, 1)
        else:
            below = pltpu.roll(jnp.where(final, p, q), 1, 1)
            above = jnp.where(final, q, pltpu.roll(q, 127, 1))
        return below, above

    def run(low):
        for x in range(16):
            v = cells_of(t_ref, 3, x) / cells_of(t_ref, 0, x)
            vp = cells_of(p_ref, 3, x) / cells_of(p_ref, 0, x)
            below, above = parts(v, vp, low)
            lo_ref[x] = 0.5 * (below + v)
            hi_ref[x] = 0.5 * (v + above)

        @pl.loop(0, 8)
        def _(f):
            for x in range(16):
                q, p = cells_of(t_ref, f, x), cells_of(p_ref, f, x)
                below, above = parts(q, p, low)
                d0, d1 = q - below, above - q
                h = 0.5 * limited(d0, d1)
                left, right = q + h, q - h
                if low:
                    left_below = jnp.where(first, q, pltpu.roll(left, 1, 1))
                    far = pltpu.roll(p, 126, 1)
                    right_above = jnp.where(
                        final, above - 0.5 * limited(d1, far - above), pltpu.roll(right, 127, 1)
                    )
                else:
                    far = pltpu.roll(p, 2, 1)
                    left_below = jnp.where(
                        first, below + 0.5 * limited(below - far, d0), pltpu.roll(left, 1, 1)
                    )
                    right_above = jnp.where(final, q, pltpu.roll(right, 127, 1))
                flux = upwind(hi_ref[x], left, right_above) - upwind(lo_ref[x], left_below, right)
                new = acc_ref[f, x] - DT * flux
                out_ref[f, x] = new
                if x in EDGES:
                    edge_ref[f, EDGES.index(x)] = new

    pl.when(gy == 0)(lambda: run(True))
    pl.when(gy == 1)(lambda: run(False))
    zc = GRAVITY * (((lane + gy * 128).astype(jnp.float32) + 0.5) / NZ - 0.5)
    for x in range(16):
        new = out_ref[3, x] - DT * zc * cells_of(t_ref, 0, x)
        out_ref[3, x] = new
        if x in EDGES:
            edge_ref[3, EDGES.index(x)] = new


EDGES = (0, 1, 14, 15)


def edge_kernel(t_ref, lo_ref, hi_ref, edge_ref, _, out_ref):
    def run(columns, base):
        vs = []
        for k in range(1, 5):
            vs.append(columns(1, k) / columns(0, k))
        faces = [0.5 * (vs[k] + vs[k + 1]) for k in range(3)]

        @pl.loop(0, 8)
        def _(f):
            qs = [columns(f, k) for k in range(6)]
            hs = [0.5 * limited(qs[k] - qs[k - 1], qs[k + 1] - qs[k]) for k in range(1, 5)]
            fluxes = [
                upwind(faces[k], qs[k + 1] + hs[k], qs[k + 2] - hs[k + 1]) for k in range(3)
            ]
            for k in range(2):
                out_ref[f, k] = edge_ref[f, base + k] - DT * (fluxes[k + 1] - fluxes[k])

    @pl.when(pl.program_id(0) == 0)
    def _():
        run(lambda f, k: lo_ref[f, 16 * k : 16 * k + 16] if k < 2 else cells_of(t_ref, f, k - 2), 0)

    @pl.when(pl.program_id(0) == 1)
    def _():
        run(lambda f, k: hi_ref[f, 16 * k - 64 : 16 * k - 48] if k > 3 else cells_of(t_ref, f, k + 12), 2)


def local(fields, col_cells, col_num, shear_sub):
    pieces = fields.reshape(NB, 8, 16, 128)
    lines = lax.all_to_all(pieces, "gx", 0, 0, tiled=True)
    send = pl.pallas_call(
        shift_kernel,
        out_shape=jax.ShapeDtypeStruct((NB, 192, 128), jnp.float32),
        in_specs=[SMEM, SMEM, SMEM, VMEM],
        out_specs=VMEM,
        scratch_shapes=[pltpu.VMEM((280, 128), jnp.float32)],
        compiler_params=pltpu.CompilerParams(vmem_limit_bytes=16 * 2**20),
        name="shift",
    )(col_cells, col_num, shear_sub, lines)
    t = lax.all_to_all(send, "gx", 0, 0, tiled=True)
    count = lax.axis_size("gz")
    up = [(i, (i + 1) % count) for i in range(count)]
    down = [(b, a) for a, b in up]
    by_half = t.reshape(8, 2, 192, 128)
    lo = lax.ppermute(by_half[:, 1, 160:], "gz", up)
    hi = lax.ppermute(by_half[:, 0, 160:], "gz", down)
    partner = lax.ppermute(t[:, :128], "gy", [(0, 1), (1, 0)])
    block = jax.ShapeDtypeStruct((8, 16, 16, 128), jnp.float32)
    edges = jax.ShapeDtypeStruct((8, 4, 16, 128), jnp.float32)
    cost = pl.CostEstimate(flops=20_000_000, bytes_accessed=4_000_000, transcendentals=0)
    acc = pl.pallas_call(
        inner_kernel,
        out_shape=block,
        in_specs=[VMEM],
        out_specs=VMEM,
        scratch_shapes=[
            pltpu.VMEM((16, 16, 128), jnp.float32),
            pltpu.VMEM((16, 24, 128), jnp.float32),
        ],
        compiler_params=pltpu.CompilerParams(vmem_limit_bytes=16 * 2**20),
        cost_estimate=cost,
        name="inner",
    )(t)
    out, edge = pl.pallas_call(
        height_kernel,
        out_shape=[block, edges],
        in_specs=[VMEM] * 3,
        out_specs=[VMEM] * 2,
        scratch_shapes=[pltpu.VMEM((16, 16, 128), jnp.float32)] * 2,
        compiler_params=pltpu.CompilerParams(vmem_limit_bytes=16 * 2**20),
        cost_estimate=cost,
        name="height",
    )(t, partner, acc)
    return pl.pallas_call(
        edge_kernel,
        out_shape=block,
        grid=(2,),
        in_specs=[VMEM] * 4 + [pl.BlockSpec(memory_space=pl.ANY)],
        out_specs=pl.BlockSpec((8, 2, 16, 128), lambda i: (0, 7 * i, 0, 0)),
        input_output_aliases={4: 0},
        compiler_params=pltpu.CompilerParams(vmem_limit_bytes=16 * 2**20),
        name="edge",
    )(t, lo, hi, edge, out)


def solution(mesh):
    return jax.shard_map(
        local,
        mesh=mesh,
        in_specs=(P(None, "gz", "gx", "gy"), P(), P(), P()),
        out_specs=P(None, "gz", "gx", "gy"),
        check_vma=False,
    )
```

```python
import jax
import jax.numpy as jnp
from jax import lax
from jax.experimental import pallas as pl
from jax.experimental.pallas import tpu as pltpu
from jax.sharding import PartitionSpec as P

DT = 0.2
GRAVITY = 4.0
NZ = 256
NB = 16
VMEM = pl.BlockSpec(memory_space=pltpu.VMEM)
SMEM = pl.BlockSpec(memory_space=pltpu.SMEM)


def shift_kernel(cells_ref, num_ref, shear_ref, src_ref, out_ref, line):
    gz = lax.axis_index("gz")
    last = lax.axis_size("gz") - 1
    half = lax.rem(lax.axis_index("gx"), 2)
    first_col = gz * 16 + half * 8
    shear = shear_ref[0]
    side = jnp.where(
        half == 1, jnp.where(gz == last, shear, 0), jnp.where(gz == 0, -shear, 0)
    )

    def one(col, extra, row):
        total = 64 * cells_ref[first_col + col] + num_ref[first_col + col] + extra
        cells = (total >> 6) & 255
        frac = (total & 63).astype(jnp.float32) * (1.0 / 64.0)
        line[0:8] = src_ref[15, col, 8:16]
        for b in range(16):
            line[8 + 16 * b : 24 + 16 * b] = src_ref[b, col]
        line[264:280] = src_ref[0, col]
        near = 1.0 - frac
        for m in range(32):
            start = ((8 * m - cells) & 255) + 8
            value = near * line[pl.ds(start, 8)] + frac * line[pl.ds(start - 1, 8)]
            out_ref[m // 2, pl.ds(pl.multiple_of(row + 8 * (m % 2), 8), 8)] = value

    @pl.loop(0, 8)
    def _(col):
        one(col, 0, 16 * col)

    @pl.loop(0, 2)
    def _(e):
        one(e + 6 * half, side, 160 + 16 * e)

    sub = lax.broadcasted_iota(jnp.int32, (8, 128), 0)
    top = sub < 4
    own = (sub < 2) | (sub >= 6)

    @pl.loop(0, 4)
    def _(c):
        for d in range(16):
            lo, hi = (d + 15) % 16, (d + 1) % 16
            a = pl.multiple_of(16 * c, 16)
            b = pl.multiple_of(16 * c + 64, 16)
            one_halo = jnp.where(top, out_ref[hi, pl.ds(a, 8)], out_ref[lo, pl.ds(a + 8, 8)])
            two_halo = jnp.where(top, out_ref[hi, pl.ds(b, 8)], out_ref[lo, pl.ds(b + 8, 8)])
            out_ref[d, pl.ds(pl.multiple_of(128 + 8 * c, 8), 8)] = jnp.where(
                own, one_halo, pltpu.roll(two_halo, 4, 0)
            )


def limited(a, b):
    return jnp.maximum(jnp.minimum(a, b), 0.0) + jnp.minimum(jnp.maximum(a, b), 0.0)


def upwind(a, left, right):
    return a * jnp.where(a > 0, left, right)


def cells_of(t_ref, f, x):
    return t_ref[2 * f + x // 8, 16 * (x % 8) : 16 * (x % 8) + 16]


def ring_of(t_ref, f, x):
    c = x % 4
    tile = t_ref[2 * f + x // 8, 128 + 8 * c : 136 + 8 * c]
    if x % 8 >= 4:
        tile = pltpu.roll(tile, 4, 0)
    return jnp.concatenate([tile, cells_of(t_ref, f, x)], axis=0)


EDGES = (0, 1, 14, 15)


def inner_kernel(t_ref, p_ref, out_ref, edge_ref, new_ref, ax_ref, ay_ref, lo_ref, hi_ref, sems):
    gy = lax.axis_index("gy")
    lane = lax.broadcasted_iota(jnp.int32, (16, 128), 1)
    first, final = lane == 0, lane == 127
    zc = GRAVITY * (((lane + gy * 128).astype(jnp.float32) + 0.5) / NZ - 0.5)

    def parts(q, p, low):
        if low:
            below = jnp.where(first, q, pltpu.roll(q, 1, 1))
            above = pltpu.roll(jnp.where(first, p, q), 127, 1)
        else:
            below = pltpu.roll(jnp.where(final, p, q), 1, 1)
            above = jnp.where(final, q, pltpu.roll(q, 127, 1))
        return below, above

    def z_flux(f, x, q, low):
        p = cells_of(p_ref, f, x)
        below, above = parts(q, p, low)
        d0, d1 = q - below, above - q
        h = 0.5 * limited(d0, d1)
        left, right = q + h, q - h
        if low:
            left_below = jnp.where(first, q, pltpu.roll(left, 1, 1))
            far = pltpu.roll(p, 126, 1)
            right_above = jnp.where(
                final, above - 0.5 * limited(d1, far - above), pltpu.roll(right, 127, 1)
            )
        else:
            far = pltpu.roll(p, 2, 1)
            left_below = jnp.where(
                first, below + 0.5 * limited(below - far, d0), pltpu.roll(left, 1, 1)
            )
            right_above = jnp.where(final, q, pltpu.roll(right, 127, 1))
        return upwind(hi_ref[x], left, right_above) - upwind(lo_ref[x], left_below, right)

    def run(low):
        before = None
        for x in range(16):
            density = ring_of(t_ref, 0, x)
            inverse = 1.0 / density
            vy = ring_of(t_ref, 2, x) * inverse
            ay_ref[x] = 0.5 * (vy + pltpu.roll(vy, 1, 0))
            vx = cells_of(t_ref, 1, x) * inverse[8:]
            if x:
                ax_ref[x] = 0.5 * (vx + before)
            before = vx
            vz = cells_of(t_ref, 3, x) * inverse[8:]
            vp = cells_of(p_ref, 3, x) / cells_of(p_ref, 0, x)
            below, above = parts(vz, vp, low)
            lo_ref[x] = 0.5 * (below + vz)
            hi_ref[x] = 0.5 * (vz + above)

        @pl.loop(0, 8)
        def _(f):
            qs, ds, fluxes, totals = {}, {}, {}, {}
            last = None
            weight = DT * (f == 3).astype(jnp.float32)

            def put(x):
                new = qs[x] - DT * totals[x]
                new_ref[f, x] = new
                if x in EDGES:
                    edge_ref[f, EDGES.index(x)] = new

            for x in range(16):
                ring = ring_of(t_ref, f, x)
                q = ring[8:]
                d = ring - pltpu.roll(ring, 1, 0)
                h = 0.5 * limited(d, pltpu.roll(d, 23, 0))
                flux = upwind(ay_ref[x], pltpu.roll(ring + h, 1, 0), ring - h)
                totals[x] = (pltpu.roll(flux, 23, 0) - flux)[8:] + z_flux(f, x, q, low)
                qs[x] = q
                if x >= 1:
                    ds[x] = q - qs[x - 1]
                if x >= 2:
                    h = 0.5 * limited(ds[x - 1], ds[x])
                    if x >= 3:
                        fluxes[x - 1] = upwind(ax_ref[x - 1], last, qs[x - 1] - h)
                    last = qs[x - 1] + h
                if x >= 4:
                    totals[x - 2] += fluxes[x - 1] - fluxes[x - 2]
                if x >= 2:
                    put(x - 2)
            put(14)
            put(15)

            @pl.when(f == 3)
            def _():
                for x in range(16):
                    new = new_ref[3, x] - DT * zc * cells_of(t_ref, 0, x)
                    new_ref[3, x] = new
                    if x in EDGES:
                        edge_ref[3, EDGES.index(x)] = new

            pltpu.make_async_copy(new_ref.at[f], out_ref.at[f], sems.at[f]).start()

    pl.when(gy == 0)(lambda: run(True))
    pl.when(gy == 1)(lambda: run(False))
    for f in range(8):
        pltpu.make_async_copy(new_ref.at[f], out_ref.at[f], sems.at[f]).wait()


def edge_kernel(t_ref, lo_ref, hi_ref, edge_ref, _, out_ref, new_ref, sems):
    copies = []
    for side in range(2):
        def columns(f, k, side=side):
            if side == 0:
                return lo_ref[f, 16 * k : 16 * k + 16] if k < 2 else cells_of(t_ref, f, k - 2)
            return hi_ref[f, 16 * k - 64 : 16 * k - 48] if k > 3 else cells_of(t_ref, f, k + 12)

        vs = [columns(1, k) / columns(0, k) for k in range(1, 5)]
        faces = [0.5 * (vs[k] + vs[k + 1]) for k in range(3)]
        for f in range(8):
            qs = [columns(f, k) for k in range(6)]
            hs = [0.5 * limited(qs[k] - qs[k - 1], qs[k + 1] - qs[k]) for k in range(1, 5)]
            fluxes = [
                upwind(faces[k], qs[k + 1] + hs[k], qs[k + 2] - hs[k + 1]) for k in range(3)
            ]
            for k in range(2):
                new_ref[side, f, k] = edge_ref[f, 2 * side + k] - DT * (fluxes[k + 1] - fluxes[k])
        copy = pltpu.make_async_copy(
            new_ref.at[side], out_ref.at[:, 14 * side : 14 * side + 2], sems.at[side]
        )
        copy.start()
        copies.append(copy)
    for copy in copies:
        copy.wait()


def local(fields, col_cells, col_num, shear_sub):
    pieces = fields.reshape(NB, 8, 16, 128)
    lines = lax.all_to_all(pieces, "gx", 0, 0, tiled=True)
    send = pl.pallas_call(
        shift_kernel,
        out_shape=jax.ShapeDtypeStruct((NB, 192, 128), jnp.float32),
        in_specs=[SMEM, SMEM, SMEM, VMEM],
        out_specs=VMEM,
        scratch_shapes=[pltpu.VMEM((280, 128), jnp.float32)],
        compiler_params=pltpu.CompilerParams(vmem_limit_bytes=16 * 2**20),
        name="shift",
    )(col_cells, col_num, shear_sub, lines)
    t = lax.all_to_all(send, "gx", 0, 0, tiled=True)
    count = lax.axis_size("gz")
    up = [(i, (i + 1) % count) for i in range(count)]
    down = [(b, a) for a, b in up]
    by_half = t.reshape(8, 2, 192, 128)
    lo = lax.ppermute(by_half[:, 1, 160:], "gz", up)
    hi = lax.ppermute(by_half[:, 0, 160:], "gz", down)
    partner = lax.ppermute(t[:, :128], "gy", [(0, 1), (1, 0)])
    block = jax.ShapeDtypeStruct((8, 16, 16, 128), jnp.float32)
    edges = jax.ShapeDtypeStruct((8, 4, 16, 128), jnp.float32)
    out, edge = pl.pallas_call(
        inner_kernel,
        out_shape=[block, edges],
        in_specs=[VMEM] * 2,
        out_specs=[pl.BlockSpec(memory_space=pl.ANY), VMEM],
        scratch_shapes=[
            pltpu.VMEM((8, 16, 16, 128), jnp.float32),
            pltpu.VMEM((16, 16, 128), jnp.float32),
            pltpu.VMEM((16, 24, 128), jnp.float32),
            pltpu.VMEM((16, 16, 128), jnp.float32),
            pltpu.VMEM((16, 16, 128), jnp.float32),
            pltpu.SemaphoreType.DMA((8,)),
        ],
        compiler_params=pltpu.CompilerParams(vmem_limit_bytes=16 * 2**20),
        cost_estimate=pl.CostEstimate(flops=40_000_000, bytes_accessed=6_000_000, transcendentals=0),
        name="inner",
    )(t, partner)
    return pl.pallas_call(
        edge_kernel,
        out_shape=block,
        in_specs=[VMEM] * 4 + [pl.BlockSpec(memory_space=pl.ANY)],
        out_specs=pl.BlockSpec(memory_space=pl.ANY),
        scratch_shapes=[
            pltpu.VMEM((2, 8, 2, 16, 128), jnp.float32),
            pltpu.SemaphoreType.DMA((2,)),
        ],
        input_output_aliases={4: 0},
        compiler_params=pltpu.CompilerParams(vmem_limit_bytes=16 * 2**20),
        name="edge",
    )(t, lo, hi, edge, out)


def solution(mesh):
    return jax.shard_map(
        local,
        mesh=mesh,
        in_specs=(P(None, "gz", "gx", "gy"), P(), P(), P()),
        out_specs=P(None, "gz", "gx", "gy"),
        check_vma=False,
    )
```

```python
import jax
import jax.numpy as jnp
from jax import lax
from jax.experimental import pallas as pl
from jax.experimental.pallas import tpu as pltpu
from jax.sharding import PartitionSpec as P

DT = 0.2
GRAVITY = 4.0
NZ = 256
NB = 16
VMEM = pl.BlockSpec(memory_space=pltpu.VMEM)
SMEM = pl.BlockSpec(memory_space=pltpu.SMEM)


def shift_kernel(cells_ref, num_ref, shear_ref, src_ref, out_ref, line, total_ref):
    gz = lax.axis_index("gz")
    last = lax.axis_size("gz") - 1
    half = lax.rem(lax.axis_index("gx"), 2)
    first_col = gz * 16 + half * 8
    shear = shear_ref[0]
    side = jnp.where(
        half == 1, jnp.where(gz == last, shear, 0), jnp.where(gz == 0, -shear, 0)
    )
    totals = (64 * cells_ref[...] + num_ref[...]).reshape(1, 128).astype(jnp.float32)
    place = lax.broadcasted_iota(jnp.int32, (1, 128), 1) - first_col
    for c in range(8):
        total_ref[c] = jnp.sum(jnp.where(place == c, totals, 0.0)).astype(jnp.int32)

    def one(col, extra, row):
        total = total_ref[col] + extra
        cells = (total >> 6) & 255
        frac = (total & 63).astype(jnp.float32) * (1.0 / 64.0)
        near = 1.0 - frac
        line[0:8] = src_ref[15, col, 8:16]
        for b in range(16):
            line[8 + 16 * b : 24 + 16 * b] = src_ref[b, col]
        line[264:280] = src_ref[0, col]
        for d in range(16):
            start = ((16 * d - cells) & 255) + 8
            out_ref[d, pl.ds(pl.multiple_of(row, 16), 16)] = (
                near * line[pl.ds(start, 16)] + frac * line[pl.ds(start - 1, 16)]
            )

    @pl.loop(0, 8)
    def _(col):
        one(col, 0, 16 * col)

    @pl.loop(0, 2)
    def _(e):
        one(e + 6 * half, side, 160 + 16 * e)

    sub = lax.broadcasted_iota(jnp.int32, (8, 128), 0)
    top = sub < 4
    own = (sub < 2) | (sub >= 6)

    @pl.loop(0, 4)
    def _(c):
        for d in range(16):
            lo, hi = (d + 15) % 16, (d + 1) % 16
            a = pl.multiple_of(16 * c, 16)
            b = pl.multiple_of(16 * c + 64, 16)
            one_halo = jnp.where(top, out_ref[hi, pl.ds(a, 8)], out_ref[lo, pl.ds(a + 8, 8)])
            two_halo = jnp.where(top, out_ref[hi, pl.ds(b, 8)], out_ref[lo, pl.ds(b + 8, 8)])
            out_ref[d, pl.ds(pl.multiple_of(128 + 8 * c, 8), 8)] = jnp.where(
                own, one_halo, pltpu.roll(two_halo, 4, 0)
            )


def limited(a, b):
    return jnp.maximum(jnp.minimum(a, b), 0.0) + jnp.minimum(jnp.maximum(a, b), 0.0)


def upwind(a, left, right):
    return a * jnp.where(a > 0, left, right)


def cells_of(t_ref, f, x):
    return t_ref[2 * f + x // 8, 16 * (x % 8) : 16 * (x % 8) + 16]


def ring_of(t_ref, f, x):
    c = x % 4
    tile = t_ref[2 * f + x // 8, 128 + 8 * c : 136 + 8 * c]
    if x % 8 >= 4:
        tile = pltpu.roll(tile, 4, 0)
    return jnp.concatenate([tile, cells_of(t_ref, f, x)], axis=0)


def inner_kernel(t_ref, p_ref, new_ref, ax_ref, ay_ref, lo_ref, hi_ref):
    gy = lax.axis_index("gy")
    lane = lax.broadcasted_iota(jnp.int32, (16, 128), 1)
    first, final = lane == 0, lane == 127
    zc = GRAVITY * (((lane + gy * 128).astype(jnp.float32) + 0.5) / NZ - 0.5)

    def parts(q, p, low):
        if low:
            below = jnp.where(first, q, pltpu.roll(q, 1, 1))
            above = pltpu.roll(jnp.where(first, p, q), 127, 1)
        else:
            below = pltpu.roll(jnp.where(final, p, q), 1, 1)
            above = jnp.where(final, q, pltpu.roll(q, 127, 1))
        return below, above

    def z_flux(f, x, q, low):
        p = cells_of(p_ref, f, x)
        below, above = parts(q, p, low)
        d0, d1 = q - below, above - q
        h = 0.5 * limited(d0, d1)
        left, right = q + h, q - h
        if low:
            left_below = jnp.where(first, q, pltpu.roll(left, 1, 1))
            far = pltpu.roll(p, 126, 1)
            right_above = jnp.where(
                final, above - 0.5 * limited(d1, far - above), pltpu.roll(right, 127, 1)
            )
        else:
            far = pltpu.roll(p, 2, 1)
            left_below = jnp.where(
                first, below + 0.5 * limited(below - far, d0), pltpu.roll(left, 1, 1)
            )
            right_above = jnp.where(final, q, pltpu.roll(right, 127, 1))
        return upwind(hi_ref[x], left, right_above) - upwind(lo_ref[x], left_below, right)

    def run(low):
        before = None
        for x in range(16):
            density = ring_of(t_ref, 0, x)
            inverse = 1.0 / density
            vy = ring_of(t_ref, 2, x) * inverse
            ay_ref[x] = 0.5 * (vy + pltpu.roll(vy, 1, 0))
            vx = cells_of(t_ref, 1, x) * inverse[8:]
            if x:
                ax_ref[x] = 0.5 * (vx + before)
            before = vx
            vz = cells_of(t_ref, 3, x) * inverse[8:]
            vp = cells_of(p_ref, 3, x) / cells_of(p_ref, 0, x)
            below, above = parts(vz, vp, low)
            lo_ref[x] = 0.5 * (below + vz)
            hi_ref[x] = 0.5 * (vz + above)

        @pl.loop(0, 8)
        def _(f):
            qs, ds, fluxes, totals = {}, {}, {}, {}
            last = None
            weight = DT * (f == 3).astype(jnp.float32)

            def put(x):
                new_ref[f, x] = qs[x] - DT * totals[x]

            for x in range(16):
                ring = ring_of(t_ref, f, x)
                q = ring[8:]
                d = ring - pltpu.roll(ring, 1, 0)
                h = 0.5 * limited(d, pltpu.roll(d, 23, 0))
                flux = upwind(ay_ref[x], pltpu.roll(ring + h, 1, 0), ring - h)
                totals[x] = (pltpu.roll(flux, 23, 0) - flux)[8:] + z_flux(f, x, q, low)
                qs[x] = q
                if x >= 1:
                    ds[x] = q - qs[x - 1]
                if x >= 2:
                    h = 0.5 * limited(ds[x - 1], ds[x])
                    if x >= 3:
                        fluxes[x - 1] = upwind(ax_ref[x - 1], last, qs[x - 1] - h)
                    last = qs[x - 1] + h
                if x >= 4:
                    totals[x - 2] += fluxes[x - 1] - fluxes[x - 2]
                if x >= 2:
                    put(x - 2)
            put(14)
            put(15)

            @pl.when(f == 3)
            def _():
                for x in range(16):
                    new_ref[3, x] = new_ref[3, x] - DT * zc * cells_of(t_ref, 0, x)

    pl.when(gy == 0)(lambda: run(True))
    pl.when(gy == 1)(lambda: run(False))


def edge_kernel(t_ref, lo_ref, hi_ref, new_ref, out_ref, edge_ref, sems):
    copy = pltpu.make_async_copy(new_ref.at[:, 2:14], out_ref.at[:, 2:14], sems.at[2])
    copy.start()
    copies = [copy]
    for side in range(2):
        def columns(f, k, side=side):
            if side == 0:
                return lo_ref[f, 16 * k : 16 * k + 16] if k < 2 else cells_of(t_ref, f, k - 2)
            return hi_ref[f, 16 * k - 64 : 16 * k - 48] if k > 3 else cells_of(t_ref, f, k + 12)

        vs = [columns(1, k) / columns(0, k) for k in range(1, 5)]
        faces = [0.5 * (vs[k] + vs[k + 1]) for k in range(3)]
        for f in range(8):
            qs = [columns(f, k) for k in range(6)]
            hs = [0.5 * limited(qs[k] - qs[k - 1], qs[k + 1] - qs[k]) for k in range(1, 5)]
            fluxes = [
                upwind(faces[k], qs[k + 1] + hs[k], qs[k + 2] - hs[k + 1]) for k in range(3)
            ]
            for k in range(2):
                edge_ref[side, f, k] = new_ref[f, 14 * side + k] - DT * (
                    fluxes[k + 1] - fluxes[k]
                )
        copy = pltpu.make_async_copy(
            edge_ref.at[side], out_ref.at[:, 14 * side : 14 * side + 2], sems.at[side]
        )
        copy.start()
        copies.append(copy)
    for copy in copies:
        copy.wait()


def local(fields, col_cells, col_num, shear_sub):
    pieces = fields.reshape(NB, 8, 16, 128)
    lines = lax.all_to_all(pieces, "gx", 0, 0, tiled=True)
    send = pl.pallas_call(
        shift_kernel,
        out_shape=jax.ShapeDtypeStruct((NB, 192, 128), jnp.float32),
        in_specs=[VMEM, VMEM, SMEM, VMEM],
        out_specs=VMEM,
        scratch_shapes=[pltpu.VMEM((280, 128), jnp.float32), pltpu.SMEM((8,), jnp.int32)],
        compiler_params=pltpu.CompilerParams(vmem_limit_bytes=16 * 2**20),
        name="shift",
    )(col_cells, col_num, shear_sub, lines)
    t = lax.all_to_all(send, "gx", 0, 0, tiled=True)
    count = lax.axis_size("gz")
    up = [(i, (i + 1) % count) for i in range(count)]
    down = [(b, a) for a, b in up]
    by_half = t.reshape(8, 2, 192, 128)
    lo = lax.ppermute(by_half[:, 1, 160:], "gz", up)
    hi = lax.ppermute(by_half[:, 0, 160:], "gz", down)
    partner = lax.ppermute(t[:, :128], "gy", [(0, 1), (1, 0)])
    block = jax.ShapeDtypeStruct((8, 16, 16, 128), jnp.float32)
    new = pl.pallas_call(
        inner_kernel,
        out_shape=block,
        in_specs=[VMEM] * 2,
        out_specs=VMEM,
        scratch_shapes=[
            pltpu.VMEM((16, 16, 128), jnp.float32),
            pltpu.VMEM((16, 24, 128), jnp.float32),
            pltpu.VMEM((16, 16, 128), jnp.float32),
            pltpu.VMEM((16, 16, 128), jnp.float32),
        ],
        compiler_params=pltpu.CompilerParams(vmem_limit_bytes=16 * 2**20),
        cost_estimate=pl.CostEstimate(flops=40_000_000, bytes_accessed=6_000_000, transcendentals=0),
        name="inner",
    )(t, partner)
    return pl.pallas_call(
        edge_kernel,
        out_shape=block,
        in_specs=[VMEM] * 4,
        out_specs=pl.BlockSpec(memory_space=pl.ANY),
        scratch_shapes=[
            pltpu.VMEM((2, 8, 2, 16, 128), jnp.float32),
            pltpu.SemaphoreType.DMA((3,)),
        ],
        compiler_params=pltpu.CompilerParams(vmem_limit_bytes=16 * 2**20),
        name="edge",
    )(t, lo, hi, new)


def solution(mesh):
    return jax.shard_map(
        local,
        mesh=mesh,
        in_specs=(P(None, "gz", "gx", "gy"), P(), P(), P()),
        out_specs=P(None, "gz", "gx", "gy"),
        check_vma=False,
    )
```

```python
import jax
import jax.numpy as jnp
from jax import lax
from jax.experimental import pallas as pl
from jax.experimental.pallas import tpu as pltpu
from jax.sharding import PartitionSpec as P

DT = 0.2
GRAVITY = 4.0
NZ = 256
NB = 16
ORDER = [9, 0, 2, 12, 11, 7, 8, 14, 10, 1, 13, 15, 3, 6, 5, 4]
PIECE = [ORDER.index(d) for d in range(NB)]
UPPER = sum((PIECE[d] % 2) << d for d in range(NB))
VMEM = pl.BlockSpec(memory_space=pltpu.VMEM)
SMEM = pl.BlockSpec(memory_space=pltpu.SMEM)


def shift_kernel(cells_ref, num_ref, shear_ref, src_ref, out_ref, line, total_ref):
    gz = lax.axis_index("gz")
    last = lax.axis_size("gz") - 1
    half = (UPPER >> lax.axis_index("gx")) & 1
    first_col = gz * 16 + half * 8
    shear = shear_ref[0]
    side = jnp.where(
        half == 1, jnp.where(gz == last, shear, 0), jnp.where(gz == 0, -shear, 0)
    )
    totals = (64 * cells_ref[...] + num_ref[...]).reshape(1, 128).astype(jnp.float32)
    place = lax.broadcasted_iota(jnp.int32, (1, 128), 1) - first_col
    for c in range(8):
        total_ref[c] = jnp.sum(jnp.where(place == c, totals, 0.0)).astype(jnp.int32)

    def one(col, extra, row):
        total = total_ref[col] + extra
        cells = (total >> 6) & 255
        frac = (total & 63).astype(jnp.float32) * (1.0 / 64.0)
        near = 1.0 - frac
        line[0:8] = src_ref[PIECE[15], col, 8:16]
        for b in range(16):
            line[8 + 16 * b : 24 + 16 * b] = src_ref[PIECE[b], col]
        line[264:280] = src_ref[PIECE[0], col]
        for d in range(16):
            start = ((16 * d - cells) & 255) + 8
            out_ref[PIECE[d], pl.ds(pl.multiple_of(row, 16), 16)] = (
                near * line[pl.ds(start, 16)] + frac * line[pl.ds(start - 1, 16)]
            )

    @pl.loop(0, 8)
    def _(col):
        one(col, 0, 16 * col)

    @pl.loop(0, 2)
    def _(e):
        one(e + 6 * half, side, 160 + 16 * e)

    sub = lax.broadcasted_iota(jnp.int32, (8, 128), 0)
    top = sub < 4
    own = (sub < 2) | (sub >= 6)

    @pl.loop(0, 4)
    def _(c):
        for d in range(16):
            lo, hi = PIECE[(d + 15) % 16], PIECE[(d + 1) % 16]
            a = pl.multiple_of(16 * c, 16)
            b = pl.multiple_of(16 * c + 64, 16)
            one_halo = jnp.where(top, out_ref[hi, pl.ds(a, 8)], out_ref[lo, pl.ds(a + 8, 8)])
            two_halo = jnp.where(top, out_ref[hi, pl.ds(b, 8)], out_ref[lo, pl.ds(b + 8, 8)])
            out_ref[PIECE[d], pl.ds(pl.multiple_of(128 + 8 * c, 8), 8)] = jnp.where(
                own, one_halo, pltpu.roll(two_halo, 4, 0)
            )


def limited(a, b):
    return jnp.maximum(jnp.minimum(a, b), 0.0) + jnp.minimum(jnp.maximum(a, b), 0.0)


def upwind(a, left, right):
    return a * jnp.where(a > 0, left, right)


def cells_of(t_ref, f, x):
    return t_ref[2 * f + x // 8, 16 * (x % 8) : 16 * (x % 8) + 16]


def ring_of(t_ref, f, x):
    c = x % 4
    tile = t_ref[2 * f + x // 8, 128 + 8 * c : 136 + 8 * c]
    if x % 8 >= 4:
        tile = pltpu.roll(tile, 4, 0)
    return jnp.concatenate([tile, cells_of(t_ref, f, x)], axis=0)


def inner_kernel(t_ref, p_ref, new_ref, ax_ref, ay_ref, lo_ref, hi_ref):
    gy = lax.axis_index("gy")
    lane = lax.broadcasted_iota(jnp.int32, (16, 128), 1)
    first, final = lane == 0, lane == 127
    zc = GRAVITY * (((lane + gy * 128).astype(jnp.float32) + 0.5) / NZ - 0.5)

    def parts(q, p, low):
        if low:
            below = jnp.where(first, q, pltpu.roll(q, 1, 1))
            above = pltpu.roll(jnp.where(first, p, q), 127, 1)
        else:
            below = pltpu.roll(jnp.where(final, p, q), 1, 1)
            above = jnp.where(final, q, pltpu.roll(q, 127, 1))
        return below, above

    def z_flux(f, x, q, low):
        p = cells_of(p_ref, f, x)
        below, above = parts(q, p, low)
        d0, d1 = q - below, above - q
        h = 0.5 * limited(d0, d1)
        left, right = q + h, q - h
        if low:
            left_below = jnp.where(first, q, pltpu.roll(left, 1, 1))
            far = pltpu.roll(p, 126, 1)
            right_above = jnp.where(
                final, above - 0.5 * limited(d1, far - above), pltpu.roll(right, 127, 1)
            )
        else:
            far = pltpu.roll(p, 2, 1)
            left_below = jnp.where(
                first, below + 0.5 * limited(below - far, d0), pltpu.roll(left, 1, 1)
            )
            right_above = jnp.where(final, q, pltpu.roll(right, 127, 1))
        return upwind(hi_ref[x], left, right_above) - upwind(lo_ref[x], left_below, right)

    def run(low):
        before = None
        for x in range(16):
            density = ring_of(t_ref, 0, x)
            inverse = 1.0 / density
            vy = ring_of(t_ref, 2, x) * inverse
            ay_ref[x] = 0.5 * (vy + pltpu.roll(vy, 1, 0))
            vx = cells_of(t_ref, 1, x) * inverse[8:]
            if x:
                ax_ref[x] = 0.5 * (vx + before)
            before = vx
            vz = cells_of(t_ref, 3, x) * inverse[8:]
            vp = cells_of(p_ref, 3, x) / cells_of(p_ref, 0, x)
            below, above = parts(vz, vp, low)
            lo_ref[x] = 0.5 * (below + vz)
            hi_ref[x] = 0.5 * (vz + above)

        @pl.loop(0, 8)
        def _(f):
            qs, ds, fluxes, totals = {}, {}, {}, {}
            last = None
            weight = DT * (f == 3).astype(jnp.float32)

            def put(x):
                new_ref[f, x] = qs[x] - DT * totals[x]

            for x in range(16):
                ring = ring_of(t_ref, f, x)
                q = ring[8:]
                d = ring - pltpu.roll(ring, 1, 0)
                h = 0.5 * limited(d, pltpu.roll(d, 23, 0))
                flux = upwind(ay_ref[x], pltpu.roll(ring + h, 1, 0), ring - h)
                totals[x] = (pltpu.roll(flux, 23, 0) - flux)[8:] + z_flux(f, x, q, low)
                qs[x] = q
                if x >= 1:
                    ds[x] = q - qs[x - 1]
                if x >= 2:
                    h = 0.5 * limited(ds[x - 1], ds[x])
                    if x >= 3:
                        fluxes[x - 1] = upwind(ax_ref[x - 1], last, qs[x - 1] - h)
                    last = qs[x - 1] + h
                if x >= 4:
                    totals[x - 2] += fluxes[x - 1] - fluxes[x - 2]
                if x >= 2:
                    put(x - 2)
            put(14)
            put(15)

            @pl.when(f == 3)
            def _():
                for x in range(16):
                    new_ref[3, x] = new_ref[3, x] - DT * zc * cells_of(t_ref, 0, x)

    pl.when(gy == 0)(lambda: run(True))
    pl.when(gy == 1)(lambda: run(False))


def edge_kernel(t_ref, lo_ref, hi_ref, new_ref, out_ref, edge_ref, sems):
    copy = pltpu.make_async_copy(new_ref.at[:, 2:14], out_ref.at[:, 2:14], sems.at[2])
    copy.start()
    copies = [copy]
    for side in range(2):
        def columns(f, k, side=side):
            if side == 0:
                return lo_ref[f, 16 * k : 16 * k + 16] if k < 2 else cells_of(t_ref, f, k - 2)
            return hi_ref[f, 16 * k - 64 : 16 * k - 48] if k > 3 else cells_of(t_ref, f, k + 12)

        vs = [columns(1, k) / columns(0, k) for k in range(1, 5)]
        faces = [0.5 * (vs[k] + vs[k + 1]) for k in range(3)]
        for f in range(8):
            qs = [columns(f, k) for k in range(6)]
            hs = [0.5 * limited(qs[k] - qs[k - 1], qs[k + 1] - qs[k]) for k in range(1, 5)]
            fluxes = [
                upwind(faces[k], qs[k + 1] + hs[k], qs[k + 2] - hs[k + 1]) for k in range(3)
            ]
            for k in range(2):
                edge_ref[side, f, k] = new_ref[f, 14 * side + k] - DT * (
                    fluxes[k + 1] - fluxes[k]
                )
        copy = pltpu.make_async_copy(
            edge_ref.at[side], out_ref.at[:, 14 * side : 14 * side + 2], sems.at[side]
        )
        copy.start()
        copies.append(copy)
    for copy in copies:
        copy.wait()


def local(fields, col_cells, col_num, shear_sub):
    pieces = fields.reshape(NB, 8, 16, 128)
    lines = lax.all_to_all(pieces, "gx", 0, 0, tiled=True, axis_index_groups=[ORDER])
    send = pl.pallas_call(
        shift_kernel,
        out_shape=jax.ShapeDtypeStruct((NB, 192, 128), jnp.float32),
        in_specs=[VMEM, VMEM, SMEM, VMEM],
        out_specs=VMEM,
        scratch_shapes=[pltpu.VMEM((280, 128), jnp.float32), pltpu.SMEM((8,), jnp.int32)],
        compiler_params=pltpu.CompilerParams(vmem_limit_bytes=16 * 2**20),
        name="shift",
    )(col_cells, col_num, shear_sub, lines)
    t = lax.all_to_all(send, "gx", 0, 0, tiled=True, axis_index_groups=[ORDER])
    count = lax.axis_size("gz")
    up = [(i, (i + 1) % count) for i in range(count)]
    down = [(b, a) for a, b in up]
    by_half = t.reshape(8, 2, 192, 128)
    lo = lax.ppermute(by_half[:, 1, 160:], "gz", up)
    hi = lax.ppermute(by_half[:, 0, 160:], "gz", down)
    partner = lax.ppermute(t[:, :128], "gy", [(0, 1), (1, 0)])
    block = jax.ShapeDtypeStruct((8, 16, 16, 128), jnp.float32)
    new = pl.pallas_call(
        inner_kernel,
        out_shape=block,
        in_specs=[VMEM] * 2,
        out_specs=VMEM,
        scratch_shapes=[
            pltpu.VMEM((16, 16, 128), jnp.float32),
            pltpu.VMEM((16, 24, 128), jnp.float32),
            pltpu.VMEM((16, 16, 128), jnp.float32),
            pltpu.VMEM((16, 16, 128), jnp.float32),
        ],
        compiler_params=pltpu.CompilerParams(vmem_limit_bytes=16 * 2**20),
        cost_estimate=pl.CostEstimate(flops=40_000_000, bytes_accessed=6_000_000, transcendentals=0),
        name="inner",
    )(t, partner)
    return pl.pallas_call(
        edge_kernel,
        out_shape=block,
        in_specs=[VMEM] * 4,
        out_specs=pl.BlockSpec(memory_space=pl.ANY),
        scratch_shapes=[
            pltpu.VMEM((2, 8, 2, 16, 128), jnp.float32),
            pltpu.SemaphoreType.DMA((3,)),
        ],
        compiler_params=pltpu.CompilerParams(vmem_limit_bytes=16 * 2**20),
        name="edge",
    )(t, lo, hi, new)


def solution(mesh):
    return jax.shard_map(
        local,
        mesh=mesh,
        in_specs=(P(None, "gz", "gx", "gy"), P(), P(), P()),
        out_specs=P(None, "gz", "gx", "gy"),
        check_vma=False,
    )
```

```python
import jax
import jax.numpy as jnp
from jax import lax
from jax.experimental import pallas as pl
from jax.experimental.pallas import tpu as pltpu
from jax.sharding import PartitionSpec as P

DT = 0.2
GRAVITY = 4.0
NZ = 256
NB = 16
ORDER = [9, 0, 2, 12, 11, 7, 8, 14, 10, 1, 13, 15, 3, 6, 5, 4]
BACK = [9, 0, 2, 12, 1, 15, 8, 14, 10, 11, 13, 7, 3, 6, 5, 4]
PIECE = [ORDER.index(d) for d in range(NB)]
SEND = [BACK.index(d) for d in range(NB)]
SLOT = [BACK.index(d) for d in ORDER]
UPPER = sum((PIECE[d] % 2) << d for d in range(NB))
VMEM = pl.BlockSpec(memory_space=pltpu.VMEM)
SMEM = pl.BlockSpec(memory_space=pltpu.SMEM)


def shift_kernel(cells_ref, num_ref, shear_ref, src_ref, out_ref, line, total_ref):
    gz = lax.axis_index("gz")
    last = lax.axis_size("gz") - 1
    half = (UPPER >> lax.axis_index("gx")) & 1
    first_col = gz * 16 + half * 8
    shear = shear_ref[0]
    side = jnp.where(
        half == 1, jnp.where(gz == last, shear, 0), jnp.where(gz == 0, -shear, 0)
    )
    totals = (64 * cells_ref[...] + num_ref[...]).reshape(1, 128).astype(jnp.float32)
    place = lax.broadcasted_iota(jnp.int32, (1, 128), 1) - first_col
    for c in range(8):
        total_ref[c] = jnp.sum(jnp.where(place == c, totals, 0.0)).astype(jnp.int32)

    def one(col, extra, row):
        total = total_ref[col] + extra
        cells = (total >> 6) & 255
        frac = (total & 63).astype(jnp.float32) * (1.0 / 64.0)
        near = 1.0 - frac
        line[0:8] = src_ref[PIECE[15], col, 8:16]
        for b in range(16):
            line[8 + 16 * b : 24 + 16 * b] = src_ref[PIECE[b], col]
        line[264:280] = src_ref[PIECE[0], col]
        for d in range(16):
            start = ((16 * d - cells) & 255) + 8
            out_ref[SEND[d], pl.ds(pl.multiple_of(row, 16), 16)] = (
                near * line[pl.ds(start, 16)] + frac * line[pl.ds(start - 1, 16)]
            )

    @pl.loop(0, 8)
    def _(col):
        one(col, 0, 16 * col)

    @pl.loop(0, 2)
    def _(e):
        one(e + 6 * half, side, 160 + 16 * e)

    sub = lax.broadcasted_iota(jnp.int32, (8, 128), 0)
    top = sub < 4
    own = (sub < 2) | (sub >= 6)

    @pl.loop(0, 4)
    def _(c):
        for d in range(16):
            lo, hi = SEND[(d + 15) % 16], SEND[(d + 1) % 16]
            a = pl.multiple_of(16 * c, 16)
            b = pl.multiple_of(16 * c + 64, 16)
            one_halo = jnp.where(top, out_ref[hi, pl.ds(a, 8)], out_ref[lo, pl.ds(a + 8, 8)])
            two_halo = jnp.where(top, out_ref[hi, pl.ds(b, 8)], out_ref[lo, pl.ds(b + 8, 8)])
            out_ref[SEND[d], pl.ds(pl.multiple_of(128 + 8 * c, 8), 8)] = jnp.where(
                own, one_halo, pltpu.roll(two_halo, 4, 0)
            )


def sort_kernel(src_ref, t_ref, cells_ref, up_ref, down_ref):
    for j in range(NB):
        t_ref[j] = src_ref[SLOT[j]]
        cells_ref[j] = src_ref[SLOT[j], :128]
        (up_ref if j % 2 else down_ref)[j // 2] = src_ref[SLOT[j], 160:]


def limited(a, b):
    return jnp.maximum(jnp.minimum(a, b), 0.0) + jnp.minimum(jnp.maximum(a, b), 0.0)


def upwind(a, left, right):
    return a * jnp.where(a > 0, left, right)


def cells_of(t_ref, f, x):
    return t_ref[2 * f + x // 8, 16 * (x % 8) : 16 * (x % 8) + 16]


def ring_of(t_ref, f, x):
    c = x % 4
    tile = t_ref[2 * f + x // 8, 128 + 8 * c : 136 + 8 * c]
    if x % 8 >= 4:
        tile = pltpu.roll(tile, 4, 0)
    return jnp.concatenate([tile, cells_of(t_ref, f, x)], axis=0)


def inner_kernel(t_ref, p_ref, new_ref, ax_ref, ay_ref, lo_ref, hi_ref):
    gy = lax.axis_index("gy")
    lane = lax.broadcasted_iota(jnp.int32, (16, 128), 1)
    first, final = lane == 0, lane == 127
    zc = GRAVITY * (((lane + gy * 128).astype(jnp.float32) + 0.5) / NZ - 0.5)

    def parts(q, p, low):
        if low:
            below = jnp.where(first, q, pltpu.roll(q, 1, 1))
            above = pltpu.roll(jnp.where(first, p, q), 127, 1)
        else:
            below = pltpu.roll(jnp.where(final, p, q), 1, 1)
            above = jnp.where(final, q, pltpu.roll(q, 127, 1))
        return below, above

    def z_flux(f, x, q, low):
        p = cells_of(p_ref, f, x)
        below, above = parts(q, p, low)
        d0, d1 = q - below, above - q
        h = 0.5 * limited(d0, d1)
        left, right = q + h, q - h
        if low:
            left_below = jnp.where(first, q, pltpu.roll(left, 1, 1))
            far = pltpu.roll(p, 126, 1)
            right_above = jnp.where(
                final, above - 0.5 * limited(d1, far - above), pltpu.roll(right, 127, 1)
            )
        else:
            far = pltpu.roll(p, 2, 1)
            left_below = jnp.where(
                first, below + 0.5 * limited(below - far, d0), pltpu.roll(left, 1, 1)
            )
            right_above = jnp.where(final, q, pltpu.roll(right, 127, 1))
        return upwind(hi_ref[x], left, right_above) - upwind(lo_ref[x], left_below, right)

    def run(low):
        before = None
        for x in range(16):
            density = ring_of(t_ref, 0, x)
            inverse = 1.0 / density
            vy = ring_of(t_ref, 2, x) * inverse
            ay_ref[x] = 0.5 * (vy + pltpu.roll(vy, 1, 0))
            vx = cells_of(t_ref, 1, x) * inverse[8:]
            if x:
                ax_ref[x] = 0.5 * (vx + before)
            before = vx
            vz = cells_of(t_ref, 3, x) * inverse[8:]
            vp = cells_of(p_ref, 3, x) / cells_of(p_ref, 0, x)
            below, above = parts(vz, vp, low)
            lo_ref[x] = 0.5 * (below + vz)
            hi_ref[x] = 0.5 * (vz + above)

        @pl.loop(0, 8)
        def _(f):
            qs, ds, fluxes, totals = {}, {}, {}, {}
            last = None
            weight = DT * (f == 3).astype(jnp.float32)

            def put(x):
                new_ref[f, x] = qs[x] - DT * totals[x]

            for x in range(16):
                ring = ring_of(t_ref, f, x)
                q = ring[8:]
                d = ring - pltpu.roll(ring, 1, 0)
                h = 0.5 * limited(d, pltpu.roll(d, 23, 0))
                flux = upwind(ay_ref[x], pltpu.roll(ring + h, 1, 0), ring - h)
                totals[x] = (pltpu.roll(flux, 23, 0) - flux)[8:] + z_flux(f, x, q, low)
                qs[x] = q
                if x >= 1:
                    ds[x] = q - qs[x - 1]
                if x >= 2:
                    h = 0.5 * limited(ds[x - 1], ds[x])
                    if x >= 3:
                        fluxes[x - 1] = upwind(ax_ref[x - 1], last, qs[x - 1] - h)
                    last = qs[x - 1] + h
                if x >= 4:
                    totals[x - 2] += fluxes[x - 1] - fluxes[x - 2]
                if x >= 2:
                    put(x - 2)
            put(14)
            put(15)

            @pl.when(f == 3)
            def _():
                for x in range(16):
                    new_ref[3, x] = new_ref[3, x] - DT * zc * cells_of(t_ref, 0, x)

    pl.when(gy == 0)(lambda: run(True))
    pl.when(gy == 1)(lambda: run(False))


def edge_kernel(t_ref, lo_ref, hi_ref, new_ref, out_ref, edge_ref, sems):
    copy = pltpu.make_async_copy(new_ref.at[:, 2:14], out_ref.at[:, 2:14], sems.at[2])
    copy.start()
    copies = [copy]
    for side in range(2):
        def columns(f, k, side=side):
            if side == 0:
                return lo_ref[f, 16 * k : 16 * k + 16] if k < 2 else cells_of(t_ref, f, k - 2)
            return hi_ref[f, 16 * k - 64 : 16 * k - 48] if k > 3 else cells_of(t_ref, f, k + 12)

        vs = [columns(1, k) / columns(0, k) for k in range(1, 5)]
        faces = [0.5 * (vs[k] + vs[k + 1]) for k in range(3)]
        for f in range(8):
            qs = [columns(f, k) for k in range(6)]
            hs = [0.5 * limited(qs[k] - qs[k - 1], qs[k + 1] - qs[k]) for k in range(1, 5)]
            fluxes = [
                upwind(faces[k], qs[k + 1] + hs[k], qs[k + 2] - hs[k + 1]) for k in range(3)
            ]
            for k in range(2):
                edge_ref[side, f, k] = new_ref[f, 14 * side + k] - DT * (
                    fluxes[k + 1] - fluxes[k]
                )
        copy = pltpu.make_async_copy(
            edge_ref.at[side], out_ref.at[:, 14 * side : 14 * side + 2], sems.at[side]
        )
        copy.start()
        copies.append(copy)
    for copy in copies:
        copy.wait()


def local(fields, col_cells, col_num, shear_sub):
    pieces = fields.reshape(NB, 8, 16, 128)
    lines = lax.all_to_all(pieces, "gx", 0, 0, tiled=True, axis_index_groups=[ORDER])
    send = pl.pallas_call(
        shift_kernel,
        out_shape=jax.ShapeDtypeStruct((NB, 192, 128), jnp.float32),
        in_specs=[VMEM, VMEM, SMEM, VMEM],
        out_specs=VMEM,
        scratch_shapes=[pltpu.VMEM((280, 128), jnp.float32), pltpu.SMEM((8,), jnp.int32)],
        compiler_params=pltpu.CompilerParams(vmem_limit_bytes=16 * 2**20),
        name="shift",
    )(col_cells, col_num, shear_sub, lines)
    arrived = lax.all_to_all(send, "gx", 0, 0, tiled=True, axis_index_groups=[BACK])
    count = lax.axis_size("gz")
    up = [(i, (i + 1) % count) for i in range(count)]
    down = [(b, a) for a, b in up]
    column = jax.ShapeDtypeStruct((8, 32, 128), jnp.float32)
    t, cells, upper, lower = pl.pallas_call(
        sort_kernel,
        out_shape=[
            jax.ShapeDtypeStruct((NB, 192, 128), jnp.float32),
            jax.ShapeDtypeStruct((NB, 128, 128), jnp.float32),
            column,
            column,
        ],
        in_specs=[VMEM],
        out_specs=[VMEM] * 4,
        compiler_params=pltpu.CompilerParams(vmem_limit_bytes=16 * 2**20),
        name="sort",
    )(arrived)
    lo = lax.ppermute(upper, "gz", up)
    hi = lax.ppermute(lower, "gz", down)
    partner = lax.ppermute(cells, "gy", [(0, 1), (1, 0)])
    block = jax.ShapeDtypeStruct((8, 16, 16, 128), jnp.float32)
    new = pl.pallas_call(
        inner_kernel,
        out_shape=block,
        in_specs=[VMEM] * 2,
        out_specs=VMEM,
        scratch_shapes=[
            pltpu.VMEM((16, 16, 128), jnp.float32),
            pltpu.VMEM((16, 24, 128), jnp.float32),
            pltpu.VMEM((16, 16, 128), jnp.float32),
            pltpu.VMEM((16, 16, 128), jnp.float32),
        ],
        compiler_params=pltpu.CompilerParams(vmem_limit_bytes=16 * 2**20),
        cost_estimate=pl.CostEstimate(flops=40_000_000, bytes_accessed=6_000_000, transcendentals=0),
        name="inner",
    )(t, partner)
    return pl.pallas_call(
        edge_kernel,
        out_shape=block,
        in_specs=[VMEM] * 4,
        out_specs=pl.BlockSpec(memory_space=pl.ANY),
        scratch_shapes=[
            pltpu.VMEM((2, 8, 2, 16, 128), jnp.float32),
            pltpu.SemaphoreType.DMA((3,)),
        ],
        compiler_params=pltpu.CompilerParams(vmem_limit_bytes=16 * 2**20),
        name="edge",
    )(t, lo, hi, new)


def solution(mesh):
    return jax.shard_map(
        local,
        mesh=mesh,
        in_specs=(P(None, "gz", "gx", "gy"), P(), P(), P()),
        out_specs=P(None, "gz", "gx", "gy"),
        check_vma=False,
    )
```

```python
import jax
import jax.numpy as jnp
from jax import lax
from jax.experimental import pallas as pl
from jax.experimental.pallas import tpu as pltpu
from jax.sharding import PartitionSpec as P

DT = 0.2
GRAVITY = 4.0
NZ = 256
NB = 16
ORDER = [9, 0, 2, 12, 11, 7, 8, 14, 10, 1, 13, 15, 3, 6, 5, 4]
PIECE = [ORDER.index(d) for d in range(NB)]
UPPER = sum((PIECE[d] % 2) << d for d in range(NB))
VMEM = pl.BlockSpec(memory_space=pltpu.VMEM)
SMEM = pl.BlockSpec(memory_space=pltpu.SMEM)


def shift_kernel(cells_ref, num_ref, shear_ref, src_ref, out_ref, line, total_ref):
    gz = lax.axis_index("gz")
    last = lax.axis_size("gz") - 1
    half = (UPPER >> lax.axis_index("gx")) & 1
    first_col = gz * 16 + half * 8
    shear = shear_ref[0]
    side = jnp.where(
        half == 1, jnp.where(gz == last, shear, 0), jnp.where(gz == 0, -shear, 0)
    )
    totals = (64 * cells_ref[...] + num_ref[...]).reshape(1, 128).astype(jnp.float32)
    place = lax.broadcasted_iota(jnp.int32, (1, 128), 1) - first_col
    for c in range(8):
        total_ref[c] = jnp.sum(jnp.where(place == c, totals, 0.0)).astype(jnp.int32)

    def one(col, extra, row):
        total = total_ref[col] + extra
        cells = (total >> 6) & 255
        frac = (total & 63).astype(jnp.float32) * (1.0 / 64.0)
        near = 1.0 - frac
        line[0:8] = src_ref[PIECE[15], col, 8:16]
        for b in range(16):
            line[8 + 16 * b : 24 + 16 * b] = src_ref[PIECE[b], col]
        line[264:280] = src_ref[PIECE[0], col]
        for d in range(16):
            start = ((16 * d - cells) & 255) + 8
            out_ref[PIECE[d], pl.ds(pl.multiple_of(row, 16), 16)] = (
                near * line[pl.ds(start, 16)] + frac * line[pl.ds(start - 1, 16)]
            )

    @pl.loop(0, 8)
    def _(col):
        one(col, 0, 16 * col)

    @pl.loop(0, 2)
    def _(e):
        one(e + 6 * half, side, 160 + 16 * e)

    sub = lax.broadcasted_iota(jnp.int32, (8, 128), 0)
    top = sub < 4
    own = (sub < 2) | (sub >= 6)

    @pl.loop(0, 4, unroll=4)
    def _(c):
        for d in range(16):
            lo, hi = PIECE[(d + 15) % 16], PIECE[(d + 1) % 16]
            a = pl.multiple_of(16 * c, 16)
            b = pl.multiple_of(16 * c + 64, 16)
            one_halo = jnp.where(top, out_ref[hi, pl.ds(a, 8)], out_ref[lo, pl.ds(a + 8, 8)])
            two_halo = jnp.where(top, out_ref[hi, pl.ds(b, 8)], out_ref[lo, pl.ds(b + 8, 8)])
            out_ref[PIECE[d], pl.ds(pl.multiple_of(128 + 8 * c, 8), 8)] = jnp.where(
                own, one_halo, pltpu.roll(two_halo, 4, 0)
            )


def limited(a, b):
    return jnp.maximum(jnp.minimum(a, b), 0.0) + jnp.minimum(jnp.maximum(a, b), 0.0)


def upwind(a, left, right):
    return a * jnp.where(a > 0, left, right)


def cells_of(t_ref, f, x):
    return t_ref[2 * f + x // 8, 16 * (x % 8) : 16 * (x % 8) + 16]


def ring_of(t_ref, f, x):
    c = x % 4
    tile = t_ref[2 * f + x // 8, 128 + 8 * c : 136 + 8 * c]
    if x % 8 >= 4:
        tile = pltpu.roll(tile, 4, 0)
    return jnp.concatenate([tile, cells_of(t_ref, f, x)], axis=0)


def inner_kernel(t_ref, p_ref, new_ref, ax_ref, ay_ref, lo_ref, hi_ref):
    gy = lax.axis_index("gy")
    lane = lax.broadcasted_iota(jnp.int32, (16, 128), 1)
    first, final = lane == 0, lane == 127
    zc = GRAVITY * (((lane + gy * 128).astype(jnp.float32) + 0.5) / NZ - 0.5)

    def parts(q, p, low):
        if low:
            below = jnp.where(first, q, pltpu.roll(q, 1, 1))
            above = pltpu.roll(jnp.where(first, p, q), 127, 1)
        else:
            below = pltpu.roll(jnp.where(final, p, q), 1, 1)
            above = jnp.where(final, q, pltpu.roll(q, 127, 1))
        return below, above

    def z_flux(f, x, q, low):
        p = cells_of(p_ref, f, x)
        below, above = parts(q, p, low)
        d0, d1 = q - below, above - q
        h = 0.5 * limited(d0, d1)
        left, right = q + h, q - h
        if low:
            left_below = jnp.where(first, q, pltpu.roll(left, 1, 1))
            far = pltpu.roll(p, 126, 1)
            right_above = jnp.where(
                final, above - 0.5 * limited(d1, far - above), pltpu.roll(right, 127, 1)
            )
        else:
            far = pltpu.roll(p, 2, 1)
            left_below = jnp.where(
                first, below + 0.5 * limited(below - far, d0), pltpu.roll(left, 1, 1)
            )
            right_above = jnp.where(final, q, pltpu.roll(right, 127, 1))
        return upwind(hi_ref[x], left, right_above) - upwind(lo_ref[x], left_below, right)

    def run(low):
        before = None
        for x in range(16):
            density = ring_of(t_ref, 0, x)
            inverse = 1.0 / density
            vy = ring_of(t_ref, 2, x) * inverse
            ay_ref[x] = 0.5 * (vy + pltpu.roll(vy, 1, 0))
            vx = cells_of(t_ref, 1, x) * inverse[8:]
            if x:
                ax_ref[x] = 0.5 * (vx + before)
            before = vx
            vz = cells_of(t_ref, 3, x) * inverse[8:]
            vp = cells_of(p_ref, 3, x) / cells_of(p_ref, 0, x)
            below, above = parts(vz, vp, low)
            lo_ref[x] = 0.5 * (below + vz)
            hi_ref[x] = 0.5 * (vz + above)

        @pl.loop(0, 8)
        def _(f):
            qs, ds, fluxes, totals = {}, {}, {}, {}
            last = None
            weight = DT * (f == 3).astype(jnp.float32)

            def put(x):
                new_ref[f, x] = qs[x] - DT * totals[x]

            for x in range(16):
                ring = ring_of(t_ref, f, x)
                q = ring[8:]
                d = ring - pltpu.roll(ring, 1, 0)
                h = 0.5 * limited(d, pltpu.roll(d, 23, 0))
                flux = upwind(ay_ref[x], pltpu.roll(ring + h, 1, 0), ring - h)
                totals[x] = (pltpu.roll(flux, 23, 0) - flux)[8:] + z_flux(f, x, q, low)
                qs[x] = q
                if x >= 1:
                    ds[x] = q - qs[x - 1]
                if x >= 2:
                    h = 0.5 * limited(ds[x - 1], ds[x])
                    if x >= 3:
                        fluxes[x - 1] = upwind(ax_ref[x - 1], last, qs[x - 1] - h)
                    last = qs[x - 1] + h
                if x >= 4:
                    totals[x - 2] += fluxes[x - 1] - fluxes[x - 2]
                if x >= 2:
                    put(x - 2)
            put(14)
            put(15)

            @pl.when(f == 3)
            def _():
                for x in range(16):
                    new_ref[3, x] = new_ref[3, x] - DT * zc * cells_of(t_ref, 0, x)

    pl.when(gy == 0)(lambda: run(True))
    pl.when(gy == 1)(lambda: run(False))


def edge_kernel(t_ref, lo_ref, hi_ref, new_ref, out_ref, edge_ref, sems):
    copy = pltpu.make_async_copy(new_ref.at[:, 2:14], out_ref.at[:, 2:14], sems.at[2])
    copy.start()
    copies = [copy]
    for side in range(2):
        def columns(f, k, side=side):
            if side == 0:
                return lo_ref[f, 16 * k : 16 * k + 16] if k < 2 else cells_of(t_ref, f, k - 2)
            return hi_ref[f, 16 * k - 64 : 16 * k - 48] if k > 3 else cells_of(t_ref, f, k + 12)

        vs = [columns(1, k) / columns(0, k) for k in range(1, 5)]
        faces = [0.5 * (vs[k] + vs[k + 1]) for k in range(3)]
        for f in range(8):
            qs = [columns(f, k) for k in range(6)]
            hs = [0.5 * limited(qs[k] - qs[k - 1], qs[k + 1] - qs[k]) for k in range(1, 5)]
            fluxes = [
                upwind(faces[k], qs[k + 1] + hs[k], qs[k + 2] - hs[k + 1]) for k in range(3)
            ]
            for k in range(2):
                edge_ref[side, f, k] = new_ref[f, 14 * side + k] - DT * (
                    fluxes[k + 1] - fluxes[k]
                )
        copy = pltpu.make_async_copy(
            edge_ref.at[side], out_ref.at[:, 14 * side : 14 * side + 2], sems.at[side]
        )
        copy.start()
        copies.append(copy)
    for copy in copies:
        copy.wait()


def local(fields, col_cells, col_num, shear_sub):
    pieces = fields.reshape(NB, 8, 16, 128)
    lines = lax.all_to_all(pieces, "gx", 0, 0, tiled=True, axis_index_groups=[ORDER])
    send = pl.pallas_call(
        shift_kernel,
        out_shape=jax.ShapeDtypeStruct((NB, 192, 128), jnp.float32),
        in_specs=[VMEM, VMEM, SMEM, VMEM],
        out_specs=VMEM,
        scratch_shapes=[pltpu.VMEM((280, 128), jnp.float32), pltpu.SMEM((8,), jnp.int32)],
        compiler_params=pltpu.CompilerParams(vmem_limit_bytes=16 * 2**20),
        name="shift",
    )(col_cells, col_num, shear_sub, lines)
    t = lax.all_to_all(send, "gx", 0, 0, tiled=True, axis_index_groups=[ORDER])
    count = lax.axis_size("gz")
    up = [(i, (i + 1) % count) for i in range(count)]
    down = [(b, a) for a, b in up]
    by_half = t.reshape(8, 2, 192, 128)
    lo = lax.ppermute(by_half[:, 1, 160:], "gz", up)
    hi = lax.ppermute(by_half[:, 0, 160:], "gz", down)
    partner = lax.ppermute(t[:, :128], "gy", [(0, 1), (1, 0)])
    block = jax.ShapeDtypeStruct((8, 16, 16, 128), jnp.float32)
    new = pl.pallas_call(
        inner_kernel,
        out_shape=block,
        in_specs=[VMEM] * 2,
        out_specs=VMEM,
        scratch_shapes=[
            pltpu.VMEM((16, 16, 128), jnp.float32),
            pltpu.VMEM((16, 24, 128), jnp.float32),
            pltpu.VMEM((16, 16, 128), jnp.float32),
            pltpu.VMEM((16, 16, 128), jnp.float32),
        ],
        compiler_params=pltpu.CompilerParams(vmem_limit_bytes=16 * 2**20),
        cost_estimate=pl.CostEstimate(flops=40_000_000, bytes_accessed=6_000_000, transcendentals=0),
        name="inner",
    )(t, partner)
    return pl.pallas_call(
        edge_kernel,
        out_shape=block,
        in_specs=[VMEM] * 4,
        out_specs=pl.BlockSpec(memory_space=pl.ANY),
        scratch_shapes=[
            pltpu.VMEM((2, 8, 2, 16, 128), jnp.float32),
            pltpu.SemaphoreType.DMA((3,)),
        ],
        compiler_params=pltpu.CompilerParams(vmem_limit_bytes=16 * 2**20),
        name="edge",
    )(t, lo, hi, new)


def solution(mesh):
    return jax.shard_map(
        local,
        mesh=mesh,
        in_specs=(P(None, "gz", "gx", "gy"), P(), P(), P()),
        out_specs=P(None, "gz", "gx", "gy"),
        check_vma=False,
    )
```

```python
import jax
import jax.numpy as jnp
from jax import lax
from jax.experimental import pallas as pl
from jax.experimental.pallas import tpu as pltpu
from jax.sharding import PartitionSpec as P

DT = 0.2
GRAVITY = 4.0
NZ = 256
NB = 16
ORDER = [9, 0, 2, 12, 11, 7, 8, 14, 10, 1, 13, 15, 3, 6, 5, 4]
PIECE = [ORDER.index(d) for d in range(NB)]
UPPER = sum((PIECE[d] % 2) << d for d in range(NB))
VMEM = pl.BlockSpec(memory_space=pltpu.VMEM)
SMEM = pl.BlockSpec(memory_space=pltpu.SMEM)


def shift_kernel(cells_ref, num_ref, shear_ref, src_ref, out_ref, line, total_ref):
    gz = lax.axis_index("gz")
    last = lax.axis_size("gz") - 1
    half = (UPPER >> lax.axis_index("gx")) & 1
    first_col = gz * 16 + half * 8
    shear = shear_ref[0]
    side = jnp.where(
        half == 1, jnp.where(gz == last, shear, 0), jnp.where(gz == 0, -shear, 0)
    )
    totals = (64 * cells_ref[...] + num_ref[...]).reshape(1, 128).astype(jnp.float32)
    place = lax.broadcasted_iota(jnp.int32, (1, 128), 1) - first_col
    for c in range(8):
        total_ref[c] = jnp.sum(jnp.where(place == c, totals, 0.0)).astype(jnp.int32)

    def one(col, extra, row):
        total = total_ref[col] + extra
        cells = (total >> 6) & 255
        frac = (total & 63).astype(jnp.float32) * (1.0 / 64.0)
        near = 1.0 - frac
        line[0:8] = src_ref[PIECE[15], col, 8:16]
        for b in range(16):
            line[8 + 16 * b : 24 + 16 * b] = src_ref[PIECE[b], col]
        line[264:280] = src_ref[PIECE[0], col]
        for d in range(16):
            start = ((16 * d - cells) & 255) + 8
            out_ref[PIECE[d], pl.ds(pl.multiple_of(row, 16), 16)] = (
                near * line[pl.ds(start, 16)] + frac * line[pl.ds(start - 1, 16)]
            )

    @pl.loop(0, 8)
    def _(col):
        one(col, 0, 16 * col)

    @pl.loop(0, 2, unroll=2)
    def _(e):
        one(e + 6 * half, side, 160 + 16 * e)

    sub = lax.broadcasted_iota(jnp.int32, (8, 128), 0)
    top = sub < 4
    own = (sub < 2) | (sub >= 6)

    @pl.loop(0, 4, unroll=4)
    def _(c):
        for d in range(16):
            lo, hi = PIECE[(d + 15) % 16], PIECE[(d + 1) % 16]
            a = pl.multiple_of(16 * c, 16)
            b = pl.multiple_of(16 * c + 64, 16)
            one_halo = jnp.where(top, out_ref[hi, pl.ds(a, 8)], out_ref[lo, pl.ds(a + 8, 8)])
            two_halo = jnp.where(top, out_ref[hi, pl.ds(b, 8)], out_ref[lo, pl.ds(b + 8, 8)])
            out_ref[PIECE[d], pl.ds(pl.multiple_of(128 + 8 * c, 8), 8)] = jnp.where(
                own, one_halo, pltpu.roll(two_halo, 4, 0)
            )


def limited(a, b):
    return jnp.maximum(jnp.minimum(a, b), 0.0) + jnp.minimum(jnp.maximum(a, b), 0.0)


def upwind(a, left, right):
    return a * jnp.where(a > 0, left, right)


def cells_of(t_ref, f, x):
    return t_ref[2 * f + x // 8, 16 * (x % 8) : 16 * (x % 8) + 16]


def ring_of(t_ref, f, x):
    c = x % 4
    tile = t_ref[2 * f + x // 8, 128 + 8 * c : 136 + 8 * c]
    if x % 8 >= 4:
        tile = pltpu.roll(tile, 4, 0)
    return jnp.concatenate([tile, cells_of(t_ref, f, x)], axis=0)


def inner_kernel(t_ref, p_ref, new_ref, ax_ref, ay_ref, lo_ref, hi_ref):
    gy = lax.axis_index("gy")
    lane = lax.broadcasted_iota(jnp.int32, (16, 128), 1)
    first, final = lane == 0, lane == 127
    zc = GRAVITY * (((lane + gy * 128).astype(jnp.float32) + 0.5) / NZ - 0.5)

    def parts(q, p, low):
        if low:
            below = jnp.where(first, q, pltpu.roll(q, 1, 1))
            above = pltpu.roll(jnp.where(first, p, q), 127, 1)
        else:
            below = pltpu.roll(jnp.where(final, p, q), 1, 1)
            above = jnp.where(final, q, pltpu.roll(q, 127, 1))
        return below, above

    def z_flux(f, x, q, low):
        p = cells_of(p_ref, f, x)
        below, above = parts(q, p, low)
        d0, d1 = q - below, above - q
        h = 0.5 * limited(d0, d1)
        left, right = q + h, q - h
        if low:
            left_below = jnp.where(first, q, pltpu.roll(left, 1, 1))
            far = pltpu.roll(p, 126, 1)
            right_above = jnp.where(
                final, above - 0.5 * limited(d1, far - above), pltpu.roll(right, 127, 1)
            )
        else:
            far = pltpu.roll(p, 2, 1)
            left_below = jnp.where(
                first, below + 0.5 * limited(below - far, d0), pltpu.roll(left, 1, 1)
            )
            right_above = jnp.where(final, q, pltpu.roll(right, 127, 1))
        return upwind(hi_ref[x], left, right_above) - upwind(lo_ref[x], left_below, right)

    def run(low):
        before = None
        for x in range(16):
            density = ring_of(t_ref, 0, x)
            inverse = 1.0 / density
            vy = ring_of(t_ref, 2, x) * inverse
            ay_ref[x] = 0.5 * (vy + pltpu.roll(vy, 1, 0))
            vx = cells_of(t_ref, 1, x) * inverse[8:]
            if x:
                ax_ref[x] = 0.5 * (vx + before)
            before = vx
            vz = cells_of(t_ref, 3, x) * inverse[8:]
            vp = cells_of(p_ref, 3, x) / cells_of(p_ref, 0, x)
            below, above = parts(vz, vp, low)
            lo_ref[x] = 0.5 * (below + vz)
            hi_ref[x] = 0.5 * (vz + above)

        @pl.loop(0, 8)
        def _(f):
            qs, ds, fluxes, totals = {}, {}, {}, {}
            last = None
            weight = DT * (f == 3).astype(jnp.float32)

            def put(x):
                new_ref[f, x] = qs[x] - DT * totals[x]

            for x in range(16):
                ring = ring_of(t_ref, f, x)
                q = ring[8:]
                d = ring - pltpu.roll(ring, 1, 0)
                h = 0.5 * limited(d, pltpu.roll(d, 23, 0))
                flux = upwind(ay_ref[x], pltpu.roll(ring + h, 1, 0), ring - h)
                totals[x] = (pltpu.roll(flux, 23, 0) - flux)[8:] + z_flux(f, x, q, low)
                qs[x] = q
                if x >= 1:
                    ds[x] = q - qs[x - 1]
                if x >= 2:
                    h = 0.5 * limited(ds[x - 1], ds[x])
                    if x >= 3:
                        fluxes[x - 1] = upwind(ax_ref[x - 1], last, qs[x - 1] - h)
                    last = qs[x - 1] + h
                if x >= 4:
                    totals[x - 2] += fluxes[x - 1] - fluxes[x - 2]
                if x >= 2:
                    put(x - 2)
            put(14)
            put(15)

            @pl.when(f == 3)
            def _():
                for x in range(16):
                    new_ref[3, x] = new_ref[3, x] - DT * zc * cells_of(t_ref, 0, x)

    pl.when(gy == 0)(lambda: run(True))
    pl.when(gy == 1)(lambda: run(False))


def edge_kernel(t_ref, lo_ref, hi_ref, new_ref, out_ref, edge_ref, sems):
    copy = pltpu.make_async_copy(new_ref.at[:, 2:14], out_ref.at[:, 2:14], sems.at[2])
    copy.start()
    copies = [copy]
    for side in range(2):
        def columns(f, k, side=side):
            if side == 0:
                return lo_ref[f, 16 * k : 16 * k + 16] if k < 2 else cells_of(t_ref, f, k - 2)
            return hi_ref[f, 16 * k - 64 : 16 * k - 48] if k > 3 else cells_of(t_ref, f, k + 12)

        vs = [columns(1, k) / columns(0, k) for k in range(1, 5)]
        faces = [0.5 * (vs[k] + vs[k + 1]) for k in range(3)]
        for f in range(8):
            qs = [columns(f, k) for k in range(6)]
            hs = [0.5 * limited(qs[k] - qs[k - 1], qs[k + 1] - qs[k]) for k in range(1, 5)]
            fluxes = [
                upwind(faces[k], qs[k + 1] + hs[k], qs[k + 2] - hs[k + 1]) for k in range(3)
            ]
            for k in range(2):
                edge_ref[side, f, k] = new_ref[f, 14 * side + k] - DT * (
                    fluxes[k + 1] - fluxes[k]
                )
        copy = pltpu.make_async_copy(
            edge_ref.at[side], out_ref.at[:, 14 * side : 14 * side + 2], sems.at[side]
        )
        copy.start()
        copies.append(copy)
    for copy in copies:
        copy.wait()


def local(fields, col_cells, col_num, shear_sub):
    pieces = fields.reshape(NB, 8, 16, 128)
    lines = lax.all_to_all(pieces, "gx", 0, 0, tiled=True, axis_index_groups=[ORDER])
    send = pl.pallas_call(
        shift_kernel,
        out_shape=jax.ShapeDtypeStruct((NB, 192, 128), jnp.float32),
        in_specs=[VMEM, VMEM, SMEM, VMEM],
        out_specs=VMEM,
        scratch_shapes=[pltpu.VMEM((280, 128), jnp.float32), pltpu.SMEM((8,), jnp.int32)],
        compiler_params=pltpu.CompilerParams(vmem_limit_bytes=16 * 2**20),
        name="shift",
    )(col_cells, col_num, shear_sub, lines)
    t = lax.all_to_all(send, "gx", 0, 0, tiled=True, axis_index_groups=[ORDER])
    count = lax.axis_size("gz")
    up = [(i, (i + 1) % count) for i in range(count)]
    down = [(b, a) for a, b in up]
    by_half = t.reshape(8, 2, 192, 128)
    lo = lax.ppermute(by_half[:, 1, 160:], "gz", up)
    hi = lax.ppermute(by_half[:, 0, 160:], "gz", down)
    partner = lax.ppermute(t[:, :128], "gy", [(0, 1), (1, 0)])
    block = jax.ShapeDtypeStruct((8, 16, 16, 128), jnp.float32)
    new = pl.pallas_call(
        inner_kernel,
        out_shape=block,
        in_specs=[VMEM] * 2,
        out_specs=VMEM,
        scratch_shapes=[
            pltpu.VMEM((16, 16, 128), jnp.float32),
            pltpu.VMEM((16, 24, 128), jnp.float32),
            pltpu.VMEM((16, 16, 128), jnp.float32),
            pltpu.VMEM((16, 16, 128), jnp.float32),
        ],
        compiler_params=pltpu.CompilerParams(vmem_limit_bytes=16 * 2**20),
        cost_estimate=pl.CostEstimate(flops=40_000_000, bytes_accessed=6_000_000, transcendentals=0),
        name="inner",
    )(t, partner)
    return pl.pallas_call(
        edge_kernel,
        out_shape=block,
        in_specs=[VMEM] * 4,
        out_specs=pl.BlockSpec(memory_space=pl.ANY),
        scratch_shapes=[
            pltpu.VMEM((2, 8, 2, 16, 128), jnp.float32),
            pltpu.SemaphoreType.DMA((3,)),
        ],
        compiler_params=pltpu.CompilerParams(vmem_limit_bytes=16 * 2**20),
        name="edge",
    )(t, lo, hi, new)


def solution(mesh):
    return jax.shard_map(
        local,
        mesh=mesh,
        in_specs=(P(None, "gz", "gx", "gy"), P(), P(), P()),
        out_specs=P(None, "gz", "gx", "gy"),
        check_vma=False,
    )
```

```python
import jax
import jax.numpy as jnp
from jax import lax
from jax.experimental import pallas as pl
from jax.experimental.pallas import tpu as pltpu
from jax.sharding import PartitionSpec as P

DT = 0.2
GRAVITY = 4.0
NZ = 256
NB = 16
ORDER = [9, 0, 2, 12, 11, 7, 8, 14, 10, 1, 13, 15, 3, 6, 5, 4]
BACK = [9, 0, 2, 12, 1, 15, 8, 14, 10, 11, 13, 7, 3, 6, 5, 4]
PIECE = [ORDER.index(d) for d in range(NB)]
SEND = [BACK.index(d) for d in range(NB)]
SLOT = [BACK.index(d) for d in ORDER]
UPPER = sum((PIECE[d] % 2) << d for d in range(NB))
VMEM = pl.BlockSpec(memory_space=pltpu.VMEM)
SMEM = pl.BlockSpec(memory_space=pltpu.SMEM)


def shift_kernel(cells_ref, num_ref, shear_ref, src_ref, out_ref, line, total_ref):
    gz = lax.axis_index("gz")
    last = lax.axis_size("gz") - 1
    half = (UPPER >> lax.axis_index("gx")) & 1
    first_col = gz * 16 + half * 8
    shear = shear_ref[0]
    side = jnp.where(
        half == 1, jnp.where(gz == last, shear, 0), jnp.where(gz == 0, -shear, 0)
    )
    totals = (64 * cells_ref[...] + num_ref[...]).reshape(1, 128).astype(jnp.float32)
    place = lax.broadcasted_iota(jnp.int32, (1, 128), 1) - first_col
    for c in range(8):
        total_ref[c] = jnp.sum(jnp.where(place == c, totals, 0.0)).astype(jnp.int32)

    def one(col, extra, row):
        total = total_ref[col] + extra
        cells = (total >> 6) & 255
        frac = (total & 63).astype(jnp.float32) * (1.0 / 64.0)
        near = 1.0 - frac
        line[0:8] = src_ref[PIECE[15], col, 8:16]
        for b in range(16):
            line[8 + 16 * b : 24 + 16 * b] = src_ref[PIECE[b], col]
        line[264:280] = src_ref[PIECE[0], col]
        for d in range(16):
            start = ((16 * d - cells) & 255) + 8
            out_ref[SEND[d], pl.ds(pl.multiple_of(row, 16), 16)] = (
                near * line[pl.ds(start, 16)] + frac * line[pl.ds(start - 1, 16)]
            )

    @pl.loop(0, 8)
    def _(col):
        one(col, 0, 16 * col)

    @pl.loop(0, 2)
    def _(e):
        one(e + 6 * half, side, 160 + 16 * e)

    sub = lax.broadcasted_iota(jnp.int32, (8, 128), 0)
    top = sub < 4
    own = (sub < 2) | (sub >= 6)

    @pl.loop(0, 4, unroll=4)
    def _(c):
        for d in range(16):
            lo, hi = SEND[(d + 15) % 16], SEND[(d + 1) % 16]
            a = pl.multiple_of(16 * c, 16)
            b = pl.multiple_of(16 * c + 64, 16)
            one_halo = jnp.where(top, out_ref[hi, pl.ds(a, 8)], out_ref[lo, pl.ds(a + 8, 8)])
            two_halo = jnp.where(top, out_ref[hi, pl.ds(b, 8)], out_ref[lo, pl.ds(b + 8, 8)])
            out_ref[SEND[d], pl.ds(pl.multiple_of(128 + 8 * c, 8), 8)] = jnp.where(
                own, one_halo, pltpu.roll(two_halo, 4, 0)
            )


def sort_kernel(src_ref, t_ref, cells_ref, up_ref, down_ref):
    for j in range(NB):
        t_ref[j] = src_ref[SLOT[j]]
        cells_ref[j] = src_ref[SLOT[j], :128]
        (up_ref if j % 2 else down_ref)[j // 2] = src_ref[SLOT[j], 160:]


def limited(a, b):
    return jnp.maximum(jnp.minimum(a, b), 0.0) + jnp.minimum(jnp.maximum(a, b), 0.0)


def upwind(a, left, right):
    return a * jnp.where(a > 0, left, right)


def cells_of(t_ref, f, x):
    return t_ref[2 * f + x // 8, 16 * (x % 8) : 16 * (x % 8) + 16]


def ring_of(t_ref, f, x):
    c = x % 4
    tile = t_ref[2 * f + x // 8, 128 + 8 * c : 136 + 8 * c]
    if x % 8 >= 4:
        tile = pltpu.roll(tile, 4, 0)
    return jnp.concatenate([tile, cells_of(t_ref, f, x)], axis=0)


def inner_kernel(t_ref, p_ref, new_ref, ax_ref, ay_ref, lo_ref, hi_ref):
    gy = lax.axis_index("gy")
    lane = lax.broadcasted_iota(jnp.int32, (16, 128), 1)
    first, final = lane == 0, lane == 127
    zc = GRAVITY * (((lane + gy * 128).astype(jnp.float32) + 0.5) / NZ - 0.5)

    def parts(q, p, low):
        if low:
            below = jnp.where(first, q, pltpu.roll(q, 1, 1))
            above = pltpu.roll(jnp.where(first, p, q), 127, 1)
        else:
            below = pltpu.roll(jnp.where(final, p, q), 1, 1)
            above = jnp.where(final, q, pltpu.roll(q, 127, 1))
        return below, above

    def z_flux(f, x, q, low):
        p = cells_of(p_ref, f, x)
        below, above = parts(q, p, low)
        d0, d1 = q - below, above - q
        h = 0.5 * limited(d0, d1)
        left, right = q + h, q - h
        if low:
            left_below = jnp.where(first, q, pltpu.roll(left, 1, 1))
            far = pltpu.roll(p, 126, 1)
            right_above = jnp.where(
                final, above - 0.5 * limited(d1, far - above), pltpu.roll(right, 127, 1)
            )
        else:
            far = pltpu.roll(p, 2, 1)
            left_below = jnp.where(
                first, below + 0.5 * limited(below - far, d0), pltpu.roll(left, 1, 1)
            )
            right_above = jnp.where(final, q, pltpu.roll(right, 127, 1))
        return upwind(hi_ref[x], left, right_above) - upwind(lo_ref[x], left_below, right)

    def run(low):
        before = None
        for x in range(16):
            density = ring_of(t_ref, 0, x)
            inverse = 1.0 / density
            vy = ring_of(t_ref, 2, x) * inverse
            ay_ref[x] = 0.5 * (vy + pltpu.roll(vy, 1, 0))
            vx = cells_of(t_ref, 1, x) * inverse[8:]
            if x:
                ax_ref[x] = 0.5 * (vx + before)
            before = vx
            vz = cells_of(t_ref, 3, x) * inverse[8:]
            vp = cells_of(p_ref, 3, x) / cells_of(p_ref, 0, x)
            below, above = parts(vz, vp, low)
            lo_ref[x] = 0.5 * (below + vz)
            hi_ref[x] = 0.5 * (vz + above)

        @pl.loop(0, 8)
        def _(f):
            qs, ds, fluxes, totals = {}, {}, {}, {}
            last = None
            weight = DT * (f == 3).astype(jnp.float32)

            def put(x):
                new_ref[f, x] = qs[x] - DT * totals[x]

            for x in range(16):
                ring = ring_of(t_ref, f, x)
                q = ring[8:]
                d = ring - pltpu.roll(ring, 1, 0)
                h = 0.5 * limited(d, pltpu.roll(d, 23, 0))
                flux = upwind(ay_ref[x], pltpu.roll(ring + h, 1, 0), ring - h)
                totals[x] = (pltpu.roll(flux, 23, 0) - flux)[8:] + z_flux(f, x, q, low)
                qs[x] = q
                if x >= 1:
                    ds[x] = q - qs[x - 1]
                if x >= 2:
                    h = 0.5 * limited(ds[x - 1], ds[x])
                    if x >= 3:
                        fluxes[x - 1] = upwind(ax_ref[x - 1], last, qs[x - 1] - h)
                    last = qs[x - 1] + h
                if x >= 4:
                    totals[x - 2] += fluxes[x - 1] - fluxes[x - 2]
                if x >= 2:
                    put(x - 2)
            put(14)
            put(15)

            @pl.when(f == 3)
            def _():
                for x in range(16):
                    new_ref[3, x] = new_ref[3, x] - DT * zc * cells_of(t_ref, 0, x)

    pl.when(gy == 0)(lambda: run(True))
    pl.when(gy == 1)(lambda: run(False))


def edge_kernel(t_ref, lo_ref, hi_ref, new_ref, out_ref, edge_ref, sems):
    copy = pltpu.make_async_copy(new_ref.at[:, 2:14], out_ref.at[:, 2:14], sems.at[2])
    copy.start()
    copies = [copy]
    for side in range(2):
        def columns(f, k, side=side):
            if side == 0:
                return lo_ref[f, 16 * k : 16 * k + 16] if k < 2 else cells_of(t_ref, f, k - 2)
            return hi_ref[f, 16 * k - 64 : 16 * k - 48] if k > 3 else cells_of(t_ref, f, k + 12)

        vs = [columns(1, k) / columns(0, k) for k in range(1, 5)]
        faces = [0.5 * (vs[k] + vs[k + 1]) for k in range(3)]
        for f in range(8):
            qs = [columns(f, k) for k in range(6)]
            hs = [0.5 * limited(qs[k] - qs[k - 1], qs[k + 1] - qs[k]) for k in range(1, 5)]
            fluxes = [
                upwind(faces[k], qs[k + 1] + hs[k], qs[k + 2] - hs[k + 1]) for k in range(3)
            ]
            for k in range(2):
                edge_ref[side, f, k] = new_ref[f, 14 * side + k] - DT * (
                    fluxes[k + 1] - fluxes[k]
                )
        copy = pltpu.make_async_copy(
            edge_ref.at[side], out_ref.at[:, 14 * side : 14 * side + 2], sems.at[side]
        )
        copy.start()
        copies.append(copy)
    for copy in copies:
        copy.wait()


def local(fields, col_cells, col_num, shear_sub):
    pieces = fields.reshape(NB, 8, 16, 128)
    lines = lax.all_to_all(pieces, "gx", 0, 0, tiled=True, axis_index_groups=[ORDER])
    send = pl.pallas_call(
        shift_kernel,
        out_shape=jax.ShapeDtypeStruct((NB, 192, 128), jnp.float32),
        in_specs=[VMEM, VMEM, SMEM, VMEM],
        out_specs=VMEM,
        scratch_shapes=[pltpu.VMEM((280, 128), jnp.float32), pltpu.SMEM((8,), jnp.int32)],
        compiler_params=pltpu.CompilerParams(vmem_limit_bytes=16 * 2**20),
        name="shift",
    )(col_cells, col_num, shear_sub, lines)
    arrived = lax.all_to_all(send, "gx", 0, 0, tiled=True, axis_index_groups=[BACK])
    count = lax.axis_size("gz")
    up = [(i, (i + 1) % count) for i in range(count)]
    down = [(b, a) for a, b in up]
    column = jax.ShapeDtypeStruct((8, 32, 128), jnp.float32)
    t, cells, upper, lower = pl.pallas_call(
        sort_kernel,
        out_shape=[
            jax.ShapeDtypeStruct((NB, 192, 128), jnp.float32),
            jax.ShapeDtypeStruct((NB, 128, 128), jnp.float32),
            column,
            column,
        ],
        in_specs=[VMEM],
        out_specs=[VMEM] * 4,
        compiler_params=pltpu.CompilerParams(vmem_limit_bytes=16 * 2**20),
        name="sort",
    )(arrived)
    lo = lax.ppermute(upper, "gz", up)
    hi = lax.ppermute(lower, "gz", down)
    partner = lax.ppermute(cells, "gy", [(0, 1), (1, 0)])
    block = jax.ShapeDtypeStruct((8, 16, 16, 128), jnp.float32)
    new = pl.pallas_call(
        inner_kernel,
        out_shape=block,
        in_specs=[VMEM] * 2,
        out_specs=VMEM,
        scratch_shapes=[
            pltpu.VMEM((16, 16, 128), jnp.float32),
            pltpu.VMEM((16, 24, 128), jnp.float32),
            pltpu.VMEM((16, 16, 128), jnp.float32),
            pltpu.VMEM((16, 16, 128), jnp.float32),
        ],
        compiler_params=pltpu.CompilerParams(vmem_limit_bytes=16 * 2**20),
        cost_estimate=pl.CostEstimate(flops=40_000_000, bytes_accessed=6_000_000, transcendentals=0),
        name="inner",
    )(t, partner)
    return pl.pallas_call(
        edge_kernel,
        out_shape=block,
        in_specs=[VMEM] * 4,
        out_specs=pl.BlockSpec(memory_space=pl.ANY),
        scratch_shapes=[
            pltpu.VMEM((2, 8, 2, 16, 128), jnp.float32),
            pltpu.SemaphoreType.DMA((3,)),
        ],
        compiler_params=pltpu.CompilerParams(vmem_limit_bytes=16 * 2**20),
        name="edge",
    )(t, lo, hi, new)


def solution(mesh):
    return jax.shard_map(
        local,
        mesh=mesh,
        in_specs=(P(None, "gz", "gx", "gy"), P(), P(), P()),
        out_specs=P(None, "gz", "gx", "gy"),
        check_vma=False,
    )
```
